256 devices in a mesh: ri: 32 (over x_hi, z, core), occ: 8 (over x_lo, y).
Axes of the slice: x: 4 (x_hi: 2, x_lo: 2; x = x_hi * 2 + x_lo), y: 4, z: 8, core: 2. Of those that a mesh axis runs over, the one named last changes fastest.
Arguments:
- three_index: bfloat16 [32768, 32, 256], P('ri', 'occ'), may hold values from -0.4375 to 0.4375
- polar_prev: float32 [2048, 32768], P('occ', 'ri'), may hold values from -6 to 6
- states: bfloat16 [32768, 64, 256], P('ri', 'occ'), may hold values from -0.005859375 to 0.005859375
- mo_energy: float32 [1024], replicated, may hold values from -3 to -0.1
- vir_energy: float32 [256], replicated, may hold values from 0.1 to 3
- orbital_energy: float32 [256], replicated, may hold values from -3 to 3
- occ_index: int32 [32], P('occ'), may hold values from 0 to 1023
- state_index: int32 [64], P('occ'), may hold values from 0 to 1023
- slab_rows: int32 [2048], replicated, may hold values from 0 to 32767, as said below
Outputs:
- polar_panel: float32 [2048, 32768], P('occ', 'ri')
- sigma: float32 [64], P('occ')
The draws below stay inside these ranges and needn't reach their ends.
Inputs may be any that keep to these rules, and one draw needn't show every extreme that they name: `slab_rows`: entry q lies among rows b * 1024 to (b + 1) * 1024 - 1 with b = (q mod 256) // 8; the 64 entries that lie in one such block are distinct and include the block's first and last row.
All inputs are finite; a program needn't handle non-finite values.
Results may differ from the reference program's by a relative error of at most 0.0017.
Values may be sent and summed in bfloat16 or wider, within the bound.
A program may use at most 128 MiB of HBM per device.

```python
import jax
import jax.numpy as jnp
from jax import lax

P_DEV = 1024
NAUX = 32768
NOCC = 32
NVIR = 256
SQ = 8
QS = 2048
NSTATE = 64
M = 256
NMO = 1024


def draw_slab_rows(key, part):
    key = jax.random.fold_in(key, 11)
    ri_count = NAUX // P_DEV
    occ_count = QS // (SQ * ri_count)
    per_block = SQ * occ_count
    keys = jax.random.split(key, ri_count)

    def one_block(block_key):
        first_key, second_key = jax.random.split(block_key)
        inner = jax.random.permutation(first_key, P_DEV - 2)[:per_block - 2] + 1
        ends = jnp.array([0, P_DEV - 1], dtype=jnp.int32)
        picks = jnp.concatenate([ends, inner.astype(jnp.int32)])
        return jax.random.permutation(second_key, picks)
    blocks = jax.vmap(one_block)(keys)
    blocks = blocks + (jnp.arange(ri_count, dtype=jnp.int32) * P_DEV)[:, None]
    arranged = blocks.reshape(ri_count, occ_count, SQ).transpose(1, 0, 2)
    return arranged.reshape(QS).astype(jnp.int32)


def place_ends(entries, rng, least, largest):
    longest = entries.shape.index(max(entries.shape))
    spots = []
    for shift in (0, 1):
        where = [jax.random.randint(jax.random.fold_in(rng, axis), (), 0, length) for axis, length in enumerate(entries.shape)]
        where[longest] = (where[longest] + shift) % entries.shape[longest]
        spots.append(tuple(where))
    return entries.at[spots[0]].set(least).at[spots[1]].set(largest)


def steps_of(key, extent, cuts, low, top_value):
    def one(axis_at, parts):
        heights = jax.random.uniform(jax.random.fold_in(jax.random.fold_in(key, 6), axis_at), (parts,), jnp.float32, low / len(cuts), top_value / len(cuts))
        return jnp.repeat(jnp.exp(heights), extent[axis_at] // parts).reshape((-1,) + (1,) * (len(extent) - axis_at - 1))

    gain = one(*cuts[0])
    for cut in cuts[1:]:
        gain = gain * one(*cut)
    return gain


def normal_values(rng, extent, width, limit, cuts=(), held_as=jnp.bfloat16):
    drawn = jax.random.normal(rng, extent, jnp.float32) * width
    if len(cuts) > 0:
        drawn = steps_of(rng, extent, cuts, -0.22, 0.18) * drawn
    return jnp.clip(drawn, min=-limit, max=limit).astype(held_as)


def setup_inputs(seed: int = 0) -> dict:
    key_list = jax.random.split(jax.random.key(seed), 10)
    return {
        "three_index": normal_values(key_list[0], (NAUX, NOCC, NVIR), 0.07, 0.4375, ((0, 32), (1, 8))),
        "polar_prev": normal_values(key_list[1], (QS, NAUX), 1.0, 6.0, ((0, 8), (1, 32)), jnp.float32),
        "states": normal_values(key_list[2], (NAUX, NSTATE, M), 0.001, 0.005859375, ((0, 32), (1, 8))),
        "mo_energy": jnp.clip(jax.random.uniform(key_list[3], (NMO,), jnp.float32, -3.0, -0.1), -3.0, -0.1),
        "vir_energy": jnp.clip(jax.random.uniform(key_list[4], (NVIR,), jnp.float32, 0.1, 3.0), 0.1, 3.0),
        "orbital_energy": jnp.clip(jax.random.uniform(key_list[5], (M,), jnp.float32, -3.0, 3.0), -3.0, 3.0),
        "occ_index": place_ends(jax.random.randint(key_list[6], (NOCC,), 0, NMO), jax.random.fold_in(key_list[6], 1), 0, NMO - 1).astype(jnp.int32),
        "state_index": place_ends(jax.random.randint(key_list[7], (NSTATE,), 0, NMO), jax.random.fold_in(key_list[7], 1), 0, NMO - 1).astype(jnp.int32),
        "slab_rows": draw_slab_rows(jax.random.fold_in(key_list[9], 71), 0),
    }


def reference(three_index, polar_prev, states, mo_energy, vir_energy, orbital_energy, occ_index, state_index, slab_rows):
    occ_energy = mo_energy[occ_index]
    energy_gap = vir_energy[None, :] - occ_energy[:, None]
    pair_weight = 4.0 * energy_gap / (energy_gap * energy_gap + 0.25)
    picked = three_index[slab_rows].astype(jnp.float32)
    scaled = (picked * pair_weight[None]).astype(jnp.bfloat16)
    flat_scaled = scaled.reshape(QS, NOCC * NVIR).astype(jnp.float32)
    flat_three = three_index.reshape(NAUX, NOCC * NVIR).astype(jnp.float32)
    product = jnp.dot(flat_scaled, flat_three.T, precision=lax.Precision.HIGHEST)
    polar_panel = polar_prev - product
    screened = polar_panel.astype(jnp.bfloat16).astype(jnp.float32)
    state_slab = states[slab_rows]

    def one_state(state):
        slab_part = lax.dynamic_index_in_dim(state_slab, state, 1, keepdims=False).astype(jnp.float32)
        own_part = lax.dynamic_index_in_dim(states, state, 1, keepdims=False).astype(jnp.float32)
        applied = jnp.dot(screened.T, slab_part, precision=lax.Precision.HIGHEST)
        return jnp.sum(own_part * applied, axis=0)

    pair_sum = lax.map(one_state, jnp.arange(NSTATE, dtype=jnp.int32))
    state_energy = mo_energy[state_index]
    difference = state_energy[:, None] - orbital_energy[None, :]
    factor = difference / (difference * difference + 0.25)
    sigma = jnp.sum(factor * pair_sum, axis=1)
    return polar_panel, sigma
```

```python
import jax
import jax.numpy as jnp
from jax import lax
from jax.experimental import pallas as pl
from jax.experimental.pallas import tpu as pltpu
from jax.sharding import PartitionSpec as P

HI, Z, CORE, LO, YS = 2, 8, 2, 2, 4
CHUNKS = Z
LANE = 128
HALF = 16
Y_FIRST = 4

STAGES = 19
(
    RELAY, A_OPP, D_OWN, D_OPP, A_RING, A_RING2, D_RING, D_RING2, PART, SUM, PASS, PASS_Y, SUM_Y, PANEL,
    NEAR, FAR_R, FAR_L, PAIRS,
) = range(1, STAGES)
ORDER = (
    (A_RING, 1), (A_RING, 2), (A_OPP, 0), (PART, 0), (A_RING, 3), (A_RING, 4), (A_RING2, 1), (A_RING2, 2),
    (RELAY, 0), (PASS_Y, 0), (SUM_Y, 0), (SUM, 0), (PART, 1), (PART, 2), (A_RING2, 3), (D_OWN, 0),
    (A_RING2, 4), (A_RING, 5), (A_RING, 6), (PASS, 0), (PASS_Y, 1), (PANEL, 0), (PART, 3), (PASS_Y, 2),
    (PART, 4), (FAR_R, 0), (SUM_Y, 1), (A_RING2, 6), (SUM_Y, 2), (D_OPP, 0), (PASS_Y, 3), (A_RING2, 5),
    (A_RING, 7), (PASS_Y, 4), (SUM, 1), (NEAR, 0), (PART, 5), (D_RING, 2), (PART, 6), (SUM_Y, 3), (SUM_Y, 4),
    (SUM, 2), (A_RING2, 7), (D_RING, 1), (PASS, 1), (FAR_L, 0), (PART, 7), (PANEL, 1), (PASS_Y, 5), (PASS, 2),
    (D_RING2, 1), (SUM, 3), (PASS_Y, 6), (SUM, 4), (D_RING2, 2), (PANEL, 2), (D_RING, 4), (PAIRS, 0),
    (SUM_Y, 5), (D_RING, 3), (NEAR, 1), (FAR_R, 1), (PASS, 3), (SUM_Y, 6), (SUM, 5), (PASS, 4), (PASS_Y, 7),
    (FAR_R, 2), (SUM, 6), (PANEL, 3), (D_RING2, 3), (NEAR, 2), (SUM, 7), (PANEL, 4), (NEAR, 3), (D_RING2, 4),
    (PASS, 5), (FAR_L, 1), (NEAR, 4), (D_RING, 6), (SUM_Y, 7), (D_RING, 5), (PASS, 6), (PANEL, 5), (PASS, 7),
    (D_RING2, 6), (FAR_L, 2), (D_RING2, 5), (NEAR, 5), (PANEL, 6), (FAR_R, 3), (FAR_L, 3), (PANEL, 7),
    (FAR_R, 4), (NEAR, 6), (PAIRS, 1), (FAR_L, 4), (D_RING, 7), (D_RING2, 7), (NEAR, 7), (FAR_R, 5),
    (PAIRS, 2), (FAR_L, 5), (FAR_R, 6), (PAIRS, 3), (FAR_L, 6), (FAR_R, 7), (PAIRS, 4), (FAR_L, 7),
    (PAIRS, 5), (PAIRS, 6), (PAIRS, 7),
)

MESH = pl.DeviceIdType.MESH
F32 = jnp.float32
BF16 = jnp.bfloat16


def remote(src, dst, send_sem, recv_sem, target):
    return pltpu.make_async_remote_copy(
        src_ref=src, dst_ref=dst, send_sem=send_sem, recv_sem=recv_sem,
        device_id=target, device_id_type=MESH,
    )


def tile_scale(peak):
    peak = jnp.max(jnp.max(peak, axis=0, keepdims=True), axis=1, keepdims=True)
    return jnp.floor(jnp.log(jnp.maximum(peak, 1e-20) * 1.001) * 1.4426950408889634) + 1.0


def encode(blocks, message):
    peak = None
    for load in blocks:
        for lane in load.lanes:
            high = jnp.abs(load(lane))
            peak = high if peak is None else jnp.maximum(peak, high)
    exponent = tile_scale(peak)
    inverse = jnp.exp2(15.0 - exponent)
    at = 0
    for load in blocks:
        for lane in load.lanes:
            message[at] = jnp.round(load(lane) * inverse).astype(jnp.int32).astype(jnp.int16)
            at += 1
    message[at] = jnp.broadcast_to(exponent, (HALF, LANE)).astype(jnp.int32).astype(jnp.int16)


def unit(message, last):
    return jnp.exp2(message[last].astype(jnp.int32).astype(F32) - 15.0)


def decode(message, at, scale):
    return message[at].astype(jnp.int32).astype(F32) * scale


class Rows:
    def __init__(self, ref, block, first, lanes):
        self.ref, self.block, self.first, self.lanes = ref, block, first, lanes

    def __call__(self, lane):
        return self.ref[self.block, pl.ds(self.first, HALF), pl.ds(lane, LANE)]


def kernel(
    x_ref, s3_ref, prev_ref, vir_ref, orb_ref, mo_ref, occ_idx, state_idx, slab_rows,
    out_ref, sig_ref,
    cols, slab, part, x_out, x_in, y_out, y_in, m_out, m_in, n_out, n_in, p_out, p_in, w_out, w_in,
    scr, acc, sg_chip, sg_line, s_ref, wide, relayed,
    a_recv, a_sib, a_send, a_opp, d_recv, d_sib, d_send, d_opp,
    x_send, x_recv, y_send, y_recv, m_send, m_recv, n_send, n_recv, p_send, p_recv, w_send, w_recv,
    c_send, c_recv, g_send, g_recv, l_send, l_recv, r_send, r_recv,
):
    width = prev_ref.shape[1]
    x_lanes = range(0, width - Y_FIRST * LANE, LANE)
    y_lanes = range(width - Y_FIRST * LANE, width, LANE)
    x_tiles, y_tiles = len(x_lanes), len(y_lanes)
    ri, k = lax.axis_index("ri"), lax.axis_index("occ")
    core = lax.rem(ri, CORE)
    z = lax.rem(ri // CORE, Z)
    hi = ri // (CORE * Z)
    y = lax.rem(k, YS)
    lo = k // YS
    xo = 1 - lo

    def ri_at(h, zz, c):
        return (h * Z + zz) * CORE + c

    def occ_at(x, yy):
        return x * YS + yy

    up = (ri_at(hi, lax.rem(z + 1, Z), core), k)
    down = (ri_at(hi, lax.rem(z + Z - 1, Z), core), k)
    sibling = (ri_at(hi, z, 1 - core), k)
    opposite = (ri_at(1 - hi, z, core), k)
    across = (ri_at(1 - hi, z, 1 - core), k)
    partner = (ri, occ_at(xo, y))
    diagonal = (ri_at(1 - hi, z, core), occ_at(xo, y))
    y_next, y_last, y_far = lax.rem(y + 1, YS), lax.rem(y + YS - 1, YS), lax.rem(y + 2, YS)
    right, left = (ri, occ_at(lo, y_next)), (ri, occ_at(lo, y_last))
    line = [(ri_at(hi, lax.rem(z + s, Z), core), k) for s in range(1, Z)]

    barrier = pltpu.get_barrier_semaphore()
    friends = [sibling, opposite, across, partner, diagonal, right, left] + line
    for friend in friends:
        pl.semaphore_signal(barrier, inc=1, device_id=friend, device_id_type=MESH)

    per_sub = prev_ref.shape[0] // (HI * Z * CORE)
    picks = LO * YS * per_sub
    groups = []
    for kk in range(LO * YS):
        spot = lax.broadcasted_iota(jnp.int32, (per_sub, LANE), 0)
        rows = jnp.zeros((per_sub, LANE), jnp.int32)
        for s in range(per_sub):
            row = slab_rows[kk * prev_ref.shape[0] + ri * per_sub + s] - ri * x_ref.shape[0]
            rows = jnp.where(spot == s, row, rows)
        groups.append(rows)
    rows = jnp.concatenate(groups, axis=0)
    place = lax.broadcasted_iota(jnp.int32, (picks, LANE), 1)
    chosen = jnp.concatenate(
        [jnp.where(place + lane == rows, 1.0, 0.0) for lane in range(0, x_ref.shape[0], LANE)], axis=1
    ).astype(BF16)
    weights = []
    for i in range(occ_idx.shape[0]):
        gap = vir_ref[...] - mo_ref[occ_idx[i]]
        weights.append(4.0 * gap / (gap * gap + 0.25))
    weight = jnp.concatenate(weights, axis=1)
    picked = jnp.dot(chosen, x_ref[...], preferred_element_type=F32)
    cols[z, core, hi] = (picked * weight).astype(BF16)

    pl.semaphore_wait(barrier, len(friends))

    a_set = (cols, a_recv, a_sib, a_send, a_opp)
    d_set = (slab, d_recv, d_sib, d_send, d_opp)

    def to_opposite(group):
        buf, recv, sib, send, opp = group
        shard = buf.at[z, core, hi]
        return remote(shard, shard, opp.at[0], recv.at[z, hi], opposite)

    def to_line(group, zz, h, way):
        buf, recv, sib, send, opp = group
        shard = buf.at[zz, core, h]
        ahead = (ri_at(hi, lax.rem(z + jnp.where(way == 0, 1, Z - 1), Z), core), k)
        return remote(shard, shard, send.at[zz, h, way], recv.at[zz, h], ahead)

    def to_sibling(group, zz, h):
        buf, recv, sib, send, opp = group
        shard = buf.at[zz, core, h]
        return remote(shard, shard, send.at[zz, h, 2], sib.at[zz, h], sibling)

    def await_shard(group, zz, h):
        buf, recv, sib, send, opp = group
        shard = buf.at[zz, core, h]
        remote(shard, shard, send.at[zz, h, 0], recv.at[zz, h], up).wait_recv()

    def await_sibling(group, zz):
        buf, recv, sib, send, opp = group
        for h in range(HI):
            shard = buf.at[zz, 1 - core, h]
            remote(shard, shard, send.at[zz, h, 2], sib.at[zz, h], sibling).wait_recv()

    def ring(group, c, far, act, arrive):
        zz = chunk_z(c)
        h = 1 - hi if far else hi
        way = lax.rem(c + 1, 2)
        if arrive:
            await_shard(group, zz, h)

        @pl.when(jnp.logical_or(c < 5, jnp.logical_and(c < 7, way == far)))
        def _():
            act(to_line(group, zz, h, way))

        act(to_sibling(group, zz, h))

    def start(copy):
        copy.start()

    def finish(copy):
        copy.wait_send()

    def chunk_z(t):
        return lax.rem(z + jnp.where(lax.rem(t, 2) == 1, Z - (t + 1) // 2, t // 2), Z)

    def panel_part(t):
        zz = chunk_z(t)
        await_sibling(a_set, zz)
        shards = CORE * HI
        lhs = cols[zz].reshape(shards * picks, cols.shape[-1])
        step = 256
        for first in range(0, width, step):
            res = lax.dot_general(
                lhs, x_ref[pl.ds(first, step), :], (((1,), (1,)), ((), ())),
                preferred_element_type=F32,
            )
            for kk in range(LO * YS):
                for g in range(shards):
                    part[t * (LO * YS) + kk, pl.ds(g * 8, 8), pl.ds(first, step)] = res[
                        g * picks + kk * 8 : g * picks + kk * 8 + 8
                    ]
        for way in range(2):
            beside = (y_next, y_last)[way]
            blocks = [Rows(part, at(t, lx, y_far), way * HALF, y_lanes) for lx in range(LO)]
            blocks += [Rows(part, at(t, lx, beside), (1 - way) * HALF, y_lanes) for lx in range(LO)]
            encode(blocks, n_out.at[t, way])
            n_copy(t, way).start()
        blocks = []
        for yy in range(YS):
            for first in (0, HALF):
                blocks.append(Rows(part, at(t, xo, yy), first, x_lanes))
        encode(blocks, x_out.at[t])
        x_copy(t).start()

    def n_copy(t, way):
        return remote(
            n_out.at[t, way], n_in.at[t, way], n_send.at[t, way], n_recv.at[t, way], (right, left)[way]
        )

    def p_copy(t, way):
        return remote(
            p_out.at[t, way], p_in.at[t, way], p_send.at[t, way], p_recv.at[t, way], (right, left)[way]
        )

    def w_copy(t):
        return remote(w_out.at[t], w_in.at[t], w_send.at[t], w_recv.at[t], partner)

    def x_copy(t):
        return remote(x_out.at[t], x_in.at[t], x_send.at[t], x_recv.at[t], partner)

    def y_copy(t, way):
        return remote(
            y_out.at[t, way], y_in.at[t, way], y_send.at[t, way], y_recv.at[t, way], (right, left)[way]
        )

    def m_copy(t, way):
        return remote(
            m_out.at[t, way], m_in.at[t, way], m_send.at[t, way], m_recv.at[t, way], (right, left)[way]
        )

    def c_copy(t, block, lane, target):
        spot = scr.at[t, block]
        return remote(spot, spot, c_send.at[t, lane], c_recv.at[t, block], target)

    def at(t, lx, yy):
        return t * (LO * YS) + occ_at(lx, yy)

    def add(block, first, lanes, message, tile, scale):
        for lane in lanes:
            spot = (block, pl.ds(first, HALF), pl.ds(lane, LANE))
            part[spot] = part[spot] + decode(message, tile, scale)
            tile += 1

    def pair_sum(t):
        x_copy(t).wait_recv()
        message = x_in.at[t]
        scale = unit(message, YS * 2 * x_tiles)
        for yy in range(YS):
            for half in range(2):
                add(at(t, lo, yy), half * HALF, x_lanes, message, (yy * 2 + half) * x_tiles, scale)
        for way in range(2):
            beside = (y_next, y_last)[way]
            encode(
                [
                    Rows(part, at(t, lo, y_far), way * HALF, x_lanes),
                    Rows(part, at(t, lo, beside), (1 - way) * HALF, x_lanes),
                ],
                y_out.at[t, way],
            )
            y_copy(t, way).start()

    def pass_on(t):
        for way in range(2):
            beside = (y_next, y_last)[way]
            y_copy(t, way).wait_recv()
            message = y_in.at[t, way]
            add(at(t, lo, beside), way * HALF, x_lanes, message, 0, unit(message, 2 * x_tiles))
            encode([Rows(part, at(t, lo, beside), way * HALF, x_lanes)], m_out.at[t, way])
            m_copy(t, way).start()

    def pass_on_y(t):
        for way in range(2):
            beside = (y_next, y_last)[way]
            n_copy(t, way).wait_recv()
            message = n_in.at[t, way]
            scale = unit(message, 2 * LO * y_tiles)
            for lx in range(LO):
                add(at(t, lx, beside), way * HALF, y_lanes, message, lx * y_tiles, scale)
            encode(
                [Rows(part, at(t, lx, beside), way * HALF, y_lanes) for lx in range(LO)], p_out.at[t, way]
            )
            p_copy(t, way).start()

    def sum_y(t):
        for way in range(2):
            p_copy(t, way).wait_recv()
        for half in range(2):
            near, far = n_in.at[t, 1 - half], p_in.at[t, half]
            near_scale, far_scale = unit(near, 2 * LO * y_tiles), unit(far, LO * y_tiles)
            for lx in range(LO):
                add(at(t, lx, y), half * HALF, y_lanes, near, (LO + lx) * y_tiles, near_scale)
                add(at(t, lx, y), half * HALF, y_lanes, far, lx * y_tiles, far_scale)
        encode([Rows(part, at(t, xo, y), half * HALF, y_lanes) for half in range(2)], w_out.at[t])
        w_copy(t).start()

    def panel(t):
        zz = chunk_z(t)
        for way in range(2):
            m_copy(t, way).wait_recv()
        w_copy(t).wait_recv()
        other = w_in.at[t]
        other_scale = unit(other, 2 * y_tiles)
        for half in range(2):
            near, far = y_in.at[t, 1 - half], m_in.at[t, half]
            near_scale, far_scale = unit(near, 2 * x_tiles), unit(far, x_tiles)
            for lane in range(0, width, LANE):
                total = part[at(t, lo, y), pl.ds(half * HALF, HALF), pl.ds(lane, LANE)]
                tile = lane // LANE
                if tile < x_tiles:
                    total = total + decode(near, x_tiles + tile, near_scale)
                    total = total + decode(far, tile, far_scale)
                else:
                    total = total + decode(other, half * y_tiles + tile - x_tiles, other_scale)
                kept = []
                for h in range(HI):
                    row = pl.multiple_of(h * (Z * CORE * 8) + zz * (CORE * 8) + half * 8, 8)
                    value = prev_ref[pl.ds(row, 8), pl.ds(lane, LANE)] - total[h * 8 : h * 8 + 8]
                    out_ref[pl.ds(row, 8), pl.ds(lane, LANE)] = value
                    kept.append(value)
                scr[t, k, pl.ds(half * HALF, HALF), pl.ds(lane, LANE)] = jnp.concatenate(
                    kept, axis=0
                ).astype(BF16)
        c_copy(t, k, 0, partner).start()
        c_copy(t, k, 1, right).start()
        c_copy(t, k, 2, left).start()

    def await_block(t, block):
        c_copy(t, block, 0, partner).wait_recv()

    def spread_partner(t):
        block = occ_at(xo, y)
        await_block(t, block)
        c_copy(t, block, 3, right).start()
        c_copy(t, block, 4, left).start()

    def spread_right(t):
        block = occ_at(lo, y_last)
        await_block(t, block)
        c_copy(t, block, 5, right).start()

    def spread_left(t):
        block = occ_at(xo, y_next)
        await_block(t, block)
        c_copy(t, block, 6, left).start()

    def energy(t):
        zz = chunk_z(t)
        for block in (occ_at(xo, y_last), occ_at(lo, y_next), occ_at(lo, y_far), occ_at(xo, y_far)):
            await_block(t, block)
        await_sibling(d_set, zz)
        lhs = scr[t].reshape(LO * YS * 2 * HALF, width)
        step = 512
        for first in range(0, s_ref.shape[1], step):
            lanes = pl.ds(first, step)
            applied = jnp.dot(lhs, s_ref[:, lanes], preferred_element_type=F32)
            total = acc[:, lanes]
            for g in range(CORE * HI):
                rows = slab[zz, g // HI, g % HI, :, lanes].astype(F32)
                for kk in range(LO * YS):
                    at = kk * 2 * HALF + g * 8
                    total = total + applied[at : at + 8] * rows[kk * 8 : kk * 8 + 8]
            acc[:, lanes] = total

    start(to_opposite(a_set))
    start(to_line(a_set, z, hi, 0))
    start(to_line(a_set, z, hi, 1))
    start(to_sibling(a_set, z, hi))

    acc[...] = jnp.zeros_like(acc)
    states, orbitals = s3_ref.shape[1:]
    depth = wide.shape[0] // states

    def spread_states(n, carry):
        at_row = pl.multiple_of(n * depth, depth)
        for lane in range(0, orbitals, LANE):
            raw = s3_ref[pl.ds(at_row, depth), :, pl.ds(lane, LANE)].astype(F32)
            wide[...] = raw.reshape(depth * states, LANE)
            for state in range(states):
                s_ref[pl.ds(at_row, depth), pl.ds(state * orbitals + lane, LANE)] = wide[
                    pl.ds(state, depth, stride=states), :
                ].astype(BF16)
        return carry

    lax.fori_loop(0, s3_ref.shape[0] // depth, spread_states, 0)
    slab[z, core, hi] = jnp.dot(chosen, s_ref[...], preferred_element_type=F32).astype(BF16)
    start(to_sibling(d_set, z, hi))

    def to_diagonal():
        return remote(slab.at[z, core, hi], relayed, r_send.at[0], r_recv.at[0], diagonal)

    def relay_on():
        return remote(relayed, slab.at[z, core, 1 - hi], d_opp.at[0], d_recv.at[z, 1 - hi], partner)

    start(to_diagonal())

    def relay(t):
        to_diagonal().wait_recv()
        start(relay_on())

    def first_far(group):
        await_shard(group, z, 1 - hi)
        start(to_line(group, z, 1 - hi, 0))
        start(to_line(group, z, 1 - hi, 1))
        start(to_sibling(group, z, 1 - hi))

    def first_own(t):
        start(to_line(d_set, z, hi, 0))
        start(to_line(d_set, z, hi, 1))

    stages = {
        RELAY: relay,
        A_OPP: lambda t: first_far(a_set),
        D_OWN: first_own,
        D_OPP: lambda t: first_far(d_set),
        A_RING: lambda t: ring(a_set, t, 0, start, True),
        A_RING2: lambda t: ring(a_set, t, 1, start, True),
        D_RING: lambda t: ring(d_set, t, 0, start, True),
        D_RING2: lambda t: ring(d_set, t, 1, start, True),
        PART: panel_part,
        SUM: pair_sum,
        PASS: pass_on,
        PASS_Y: pass_on_y,
        SUM_Y: sum_y,
        PANEL: panel,
        NEAR: spread_partner,
        FAR_R: spread_right,
        FAR_L: spread_left,
        PAIRS: energy,
    }

    def event(n, carry):
        word = jnp.int32(0)
        for at_word in range(0, len(ORDER), 3):
            packed = 0
            for stage, t in reversed(ORDER[at_word : at_word + 3]):
                packed = packed * 256 + stage * CHUNKS + t
            word = jnp.where(n // 3 == at_word // 3, packed, word)
        place = lax.rem(n, 3)
        code = jnp.where(place == 0, word, jnp.where(place == 1, word // 256, word // 65536)) % 256
        for stage, body in stages.items():
            @pl.when(code // CHUNKS == stage)
            def _():
                body(lax.rem(code, CHUNKS))
        return carry

    lax.fori_loop(0, len(ORDER), event, 0)

    pairs = jnp.sum(acc[...], axis=0, keepdims=True)
    mine = hi * CORE + core
    for n in range(state_idx.shape[0]):
        gap = mo_ref[state_idx[n]] - orb_ref[...]
        factor = gap / (gap * gap + 0.25)
        value = jnp.sum(factor * pairs[:, n * orbitals : (n + 1) * orbitals], axis=1, keepdims=True)
        sg_chip[mine, pl.ds(n, 1), :] = jnp.broadcast_to(value, (1, LANE))

    def chip_copy(n, target):
        spot = sg_chip.at[mine]
        return remote(spot, spot, g_send.at[n], g_recv.at[mine], target)

    chip = [
        (sibling, hi * CORE + 1 - core),
        (opposite, (1 - hi) * CORE + core),
        (across, (1 - hi) * CORE + 1 - core),
    ]
    for n, (target, slot) in enumerate(chip):
        chip_copy(n, target).start()
    for n, (target, slot) in enumerate(chip):
        spot = sg_chip.at[slot]
        remote(spot, spot, g_send.at[n], g_recv.at[slot], target).wait_recv()
    sg_line[z] = (sg_chip[0] + sg_chip[1]) + (sg_chip[2] + sg_chip[3])

    def line_copy(n, target):
        spot = sg_line.at[z]
        return remote(spot, spot, l_send.at[n], l_recv.at[z], target)

    for n, target in enumerate(line):
        line_copy(n, target).start()
    for n, target in enumerate(line):
        slot = lax.rem(z + 1 + n, Z)
        spot = sg_line.at[slot]
        remote(spot, spot, l_send.at[n], l_recv.at[slot], target).wait_recv()
    total = sg_line[0]
    for n in range(1, Z):
        total = total + sg_line[n]
    diag = lax.broadcasted_iota(jnp.int32, total.shape, 0) == lax.broadcasted_iota(jnp.int32, total.shape, 1)
    sig_ref[...] = jnp.sum(jnp.where(diag, total, 0.0), axis=0, keepdims=True)[:, : sig_ref.shape[1]]

    for n, (target, slot) in enumerate(chip):
        chip_copy(n, target).wait_send()
    for n, target in enumerate(line):
        line_copy(n, target).wait_send()
    finish(to_opposite(a_set))
    finish(to_diagonal())
    finish(relay_on())
    for group in (a_set, d_set):
        for h in range(HI):
            finish(to_line(group, z, h, 0))
            finish(to_line(group, z, h, 1))
            finish(to_sibling(group, z, h))

        def finish_ring(c, carry):
            ring(group, c, 0, finish, False)
            ring(group, c, 1, finish, False)
            return carry

        lax.fori_loop(1, CHUNKS, finish_ring, 0)

    def drain(t, carry):
        x_copy(t).wait_send()
        for way in range(2):
            y_copy(t, way).wait_send()
            m_copy(t, way).wait_send()
            n_copy(t, way).wait_send()
            p_copy(t, way).wait_send()
        w_copy(t).wait_send()
        for lane in range(7):
            c_copy(t, k, lane, partner).wait_send()
        return carry

    lax.fori_loop(0, CHUNKS, drain, 0)


def local(
    three_index,
    polar_prev,
    states,
    mo_energy,
    vir_energy,
    orbital_energy,
    occ_index,
    state_index,
    slab_rows,
):
    ri_count = lax.axis_size("ri")
    occ_count = lax.axis_size("occ")
    assert (ri_count, occ_count) == (HI * Z * CORE, LO * YS)
    p_dev = three_index.shape[0]
    col_block = polar_prev.shape[0]
    picks = slab_rows.shape[0] // ri_count
    ns_dev, orbitals = states.shape[1:]
    flat = three_index.reshape(p_dev, -1)
    pairs = flat.shape[1]
    spread = ns_dev * orbitals
    y_tiles = Y_FIRST
    x_tiles = p_dev // LANE - Y_FIRST

    def message(count, *lead):
        return pltpu.VMEM((CHUNKS, *lead, count + 1, HALF, LANE), jnp.int16)

    vmem = pl.BlockSpec(memory_space=pltpu.VMEM)
    smem = pl.BlockSpec(memory_space=pltpu.SMEM)
    dma = pltpu.SemaphoreType.DMA
    ring_sems = [dma((Z, HI)), dma((Z, HI)), dma((Z, HI, 3)), dma((1,))]
    panel_out, sig = pl.pallas_call(
        kernel,
        out_shape=(
            jax.ShapeDtypeStruct((col_block, p_dev), F32),
            jax.ShapeDtypeStruct((1, ns_dev), F32),
        ),
        in_specs=[vmem] * 5 + [smem] * 4,
        out_specs=(vmem, vmem),
        scratch_shapes=[
            pltpu.VMEM((Z, CORE, HI, picks, pairs), BF16),
            pltpu.VMEM((Z, CORE, HI, picks, spread), BF16),
            pltpu.VMEM((CHUNKS * occ_count, 2 * HALF, p_dev), F32),
            message(YS * 2 * x_tiles), message(YS * 2 * x_tiles),
            message(2 * x_tiles, 2), message(2 * x_tiles, 2),
            message(x_tiles, 2), message(x_tiles, 2),
            message(2 * LO * y_tiles, 2), message(2 * LO * y_tiles, 2),
            message(LO * y_tiles, 2), message(LO * y_tiles, 2),
            message(2 * y_tiles), message(2 * y_tiles),
            pltpu.VMEM((CHUNKS, occ_count, 2 * HALF, p_dev), BF16),
            pltpu.VMEM((8, spread), F32),
            pltpu.VMEM((HI * CORE, 8, LANE), F32),
            pltpu.VMEM((Z, 8, LANE), F32),
            pltpu.VMEM((p_dev, spread), BF16),
            pltpu.VMEM((LANE * ns_dev, LANE), F32),
            pltpu.VMEM((picks, spread), BF16),
            *ring_sems,
            *ring_sems,
            dma((CHUNKS,)), dma((CHUNKS,)),
            dma((CHUNKS, 2)), dma((CHUNKS, 2)),
            dma((CHUNKS, 2)), dma((CHUNKS, 2)),
            dma((CHUNKS, 2)), dma((CHUNKS, 2)),
            dma((CHUNKS, 2)), dma((CHUNKS, 2)),
            dma((CHUNKS,)), dma((CHUNKS,)),
            dma((CHUNKS, 7)), dma((CHUNKS, occ_count)),
            dma((3,)), dma((HI * CORE,)),
            dma((Z - 1,)), dma((Z,)),
            dma((1,)), dma((1,)),
        ],
        compiler_params=pltpu.CompilerParams(
            collective_id=0, has_side_effects=True, vmem_limit_bytes=60 * 2**20
        ),
        cost_estimate=pl.CostEstimate(
            flops=13 * 10**9, bytes_accessed=9 * 2**20, transcendentals=0
        ),
    )(
        flat, states, polar_prev,
        vir_energy.reshape(1, -1), orbital_energy.reshape(1, -1),
        mo_energy, occ_index, state_index, slab_rows,
    )
    return (panel_out, sig.reshape(ns_dev))


def solution(mesh):
    in_specs = (
        P("ri", "occ", None),
        P("occ", "ri"),
        P("ri", "occ", None),
        P(),
        P(),
        P(),
        P("occ"),
        P("occ"),
        P(),
    )
    out_specs = (P("occ", "ri"), P("occ"))
    return jax.shard_map(local, mesh=mesh, in_specs=in_specs, out_specs=out_specs, check_vma=False)
```

```python
import jax
import jax.numpy as jnp
from jax import lax
from jax.experimental import pallas as pl
from jax.experimental.pallas import tpu as pltpu
from jax.sharding import PartitionSpec as P

HI, Z, CORE, LO, YS = 2, 8, 2, 2, 4
CHUNKS = Z
LANE = 128
HALF = 16
Y_FIRST = 4

(
    RELAY, A_OPP, D_PREP, D_OWN, D_OPP, A_RING, A_RING2, D_RING, D_RING2, PART_Y, PART_X, SUM, PASS, PASS_Y,
    SUM_Y, PANEL, NEAR, FAR_R, FAR_L, PAIRS,
) = range(20)
ORDER = (
    (D_PREP, 0), (A_OPP, 0), (A_RING, 1), (A_RING, 2), (PART_Y, 0), (PART_X, 0), (PASS_Y, 0), (RELAY, 0),
    (A_RING2, 1), (A_RING2, 2), (A_RING, 3), (A_RING, 4), (SUM_Y, 0), (SUM, 0), (PART_Y, 1), (PART_X, 1),
    (PART_Y, 2), (PASS, 0), (PART_X, 2), (A_RING2, 3), (A_RING2, 4), (A_RING, 5), (A_RING, 6), (PASS_Y, 1),
    (PANEL, 0), (PASS_Y, 2), (SUM_Y, 1), (PART_Y, 3), (PART_X, 3), (D_OWN, 0), (A_RING2, 6), (D_OPP, 0),
    (PART_Y, 4), (PART_X, 4), (SUM_Y, 2), (A_RING2, 5), (FAR_R, 0), (PASS_Y, 3), (A_RING, 7), (SUM, 1),
    (NEAR, 0), (PASS_Y, 4), (PART_Y, 5), (PART_X, 5), (PART_Y, 6), (PART_X, 6), (PASS, 1), (SUM_Y, 3),
    (SUM, 2), (SUM_Y, 4), (A_RING2, 7), (FAR_L, 0), (SUM, 3), (PANEL, 1), (PART_Y, 7), (PASS, 2), (PART_X, 7),
    (SUM, 4), (PASS, 3), (D_RING, 1), (D_RING2, 1), (D_RING, 2), (D_RING2, 2), (PASS_Y, 5), (PASS_Y, 6),
    (PANEL, 2), (FAR_R, 1), (PAIRS, 0, 0), (PAIRS, 0, 1), (PAIRS, 0, 2), (PAIRS, 0, 3), (PANEL, 3), (NEAR, 1),
    (SUM, 5), (PASS, 4), (PASS_Y, 7), (SUM_Y, 5), (SUM, 6), (SUM_Y, 6), (NEAR, 2), (PANEL, 4), (NEAR, 3),
    (SUM, 7), (FAR_R, 2), (PASS, 5), (D_RING, 3), (D_RING2, 3), (D_RING, 4), (D_RING2, 4), (NEAR, 4),
    (SUM_Y, 7), (FAR_L, 1), (PASS, 6), (FAR_R, 3), (FAR_L, 2), (PANEL, 5), (PASS, 7), (FAR_L, 3), (PANEL, 6),
    (NEAR, 5), (FAR_L, 4), (PAIRS, 1, 0), (FAR_R, 4), (PAIRS, 1, 1), (NEAR, 6), (PAIRS, 1, 2), (PANEL, 7),
    (PAIRS, 1, 3), (D_RING, 5), (D_RING2, 5), (D_RING, 6), (D_RING2, 6), (PAIRS, 2, 0), (PAIRS, 2, 1),
    (NEAR, 7), (PAIRS, 2, 2), (PAIRS, 2, 3), (FAR_R, 5), (PAIRS, 3, 0), (PAIRS, 3, 1), (FAR_R, 6),
    (PAIRS, 3, 2), (FAR_L, 5), (PAIRS, 3, 3), (D_RING, 7), (D_RING2, 7), (FAR_L, 6), (PAIRS, 4, 0),
    (PAIRS, 4, 1), (PAIRS, 4, 2), (FAR_L, 7), (FAR_R, 7), (PAIRS, 4, 3), (PAIRS, 5, 0), (PAIRS, 5, 1),
    (PAIRS, 5, 2), (PAIRS, 5, 3), (PAIRS, 6, 0), (PAIRS, 6, 1), (PAIRS, 6, 2), (PAIRS, 6, 3), (PAIRS, 7, 0),
    (PAIRS, 7, 1), (PAIRS, 7, 2), (PAIRS, 7, 3),
)

MESH = pl.DeviceIdType.MESH
F32 = jnp.float32
BF16 = jnp.bfloat16


def remote(src, dst, send_sem, recv_sem, target):
    return pltpu.make_async_remote_copy(
        src_ref=src, dst_ref=dst, send_sem=send_sem, recv_sem=recv_sem,
        device_id=target, device_id_type=MESH,
    )


def tile_scale(peak):
    return jnp.floor(jnp.log(jnp.maximum(peak, 1e-20) * 1.001) * 1.4426950408889634) + 1.0


def encode(blocks, message):
    peak = None
    for load in blocks:
        for lane in load.lanes:
            high = jnp.abs(load(lane))
            peak = high if peak is None else jnp.maximum(peak, high)
    exponent = tile_scale(peak)
    inverse = jnp.exp2(15.0 - exponent)
    at = 0
    for load in blocks:
        for lane in load.lanes:
            message[at] = (load(lane) * inverse).astype(jnp.int32).astype(jnp.int16)
            at += 1
    message[at] = exponent.astype(jnp.int32).astype(jnp.int16)


def unit(message, last):
    return jnp.exp2(message[last].astype(jnp.int32).astype(F32) - 15.0)


def decode(message, at, scale):
    return message[at].astype(jnp.int32).astype(F32) * scale


class Rows:
    def __init__(self, ref, block, first, lanes):
        self.ref, self.block, self.first, self.lanes = ref, block, first, lanes

    def __call__(self, lane):
        return self.ref[self.block, pl.ds(self.first, HALF), pl.ds(lane, LANE)]


def kernel(
    x_ref, s3_hbm, prev_hbm, vir_ref, orb_ref, mo_ref, occ_idx, state_idx, slab_rows,
    out_ref, sig_ref,
    cols, slab, part, x_out, x_in, y_out, y_in, m_out, m_in, n_out, n_in, p_out, p_in, w_out, w_in,
    scr, acc, sg_chip, sg_line, s_ref, wide, relayed, s3_ref, prev_ref,
    a_recv, a_sib, a_send, a_opp, d_recv, d_sib, d_send, d_opp,
    x_send, x_recv, y_send, y_recv, m_send, m_recv, n_send, n_recv, p_send, p_recv, w_send, w_recv,
    c_send, c_recv, g_send, g_recv, l_send, l_recv, r_send, r_recv, load,
):
    width = prev_ref.shape[1]
    x_lanes = range(0, width - Y_FIRST * LANE, LANE)
    y_lanes = range(width - Y_FIRST * LANE, width, LANE)
    x_tiles, y_tiles = len(x_lanes), len(y_lanes)
    ri, k = lax.axis_index("ri"), lax.axis_index("occ")
    core = lax.rem(ri, CORE)
    z = lax.rem(ri // CORE, Z)
    hi = ri // (CORE * Z)
    y = lax.rem(k, YS)
    lo = k // YS
    xo = 1 - lo

    def ri_at(h, zz, c):
        return (h * Z + zz) * CORE + c

    def occ_at(x, yy):
        return x * YS + yy

    up = (ri_at(hi, lax.rem(z + 1, Z), core), k)
    down = (ri_at(hi, lax.rem(z + Z - 1, Z), core), k)
    sibling = (ri_at(hi, z, 1 - core), k)
    opposite = (ri_at(1 - hi, z, core), k)
    across = (ri_at(1 - hi, z, 1 - core), k)
    partner = (ri, occ_at(xo, y))
    diagonal = (ri_at(1 - hi, z, core), occ_at(xo, y))
    y_next, y_last, y_far = lax.rem(y + 1, YS), lax.rem(y + YS - 1, YS), lax.rem(y + 2, YS)
    right, left = (ri, occ_at(lo, y_next)), (ri, occ_at(lo, y_last))
    line = [(ri_at(hi, lax.rem(z + s, Z), core), k) for s in range(1, Z)]

    s3_copy = pltpu.make_async_copy(s3_hbm, s3_ref, load.at[0])
    prev_copy = pltpu.make_async_copy(prev_hbm, prev_ref, load.at[1])
    barrier = pltpu.get_barrier_semaphore()
    friends = [sibling, opposite, across, partner, diagonal, right, left] + line
    for friend in friends:
        pl.semaphore_signal(barrier, inc=1, device_id=friend, device_id_type=MESH)

    s3_copy.start()
    prev_copy.start()

    per_sub = prev_ref.shape[0] // (HI * Z * CORE)
    picks = LO * YS * per_sub
    groups = []
    for kk in range(LO * YS):
        spot = lax.broadcasted_iota(jnp.int32, (per_sub, LANE), 0)
        rows = jnp.zeros((per_sub, LANE), jnp.int32)
        for s in range(per_sub):
            row = slab_rows[kk * prev_ref.shape[0] + ri * per_sub + s] - ri * x_ref.shape[0]
            rows = jnp.where(spot == s, row, rows)
        groups.append(rows)
    rows = jnp.concatenate(groups, axis=0)
    place = lax.broadcasted_iota(jnp.int32, (picks, LANE), 1)
    chosen = jnp.concatenate(
        [jnp.where(place + lane == rows, 1.0, 0.0) for lane in range(0, x_ref.shape[0], LANE)], axis=1
    ).astype(BF16)
    weights = []
    for i in range(occ_idx.shape[0]):
        gap = vir_ref[...] - mo_ref[occ_idx[i]]
        weights.append(4.0 * gap / (gap * gap + 0.25))
    weight = jnp.concatenate(weights, axis=1)
    picked = jnp.dot(chosen, x_ref[...], preferred_element_type=F32)
    cols[z, core, hi] = (picked * weight).astype(BF16)

    pl.semaphore_wait(barrier, len(friends))

    a_set = (cols, a_recv, a_sib, a_send, a_opp)
    d_set = (slab, d_recv, d_sib, d_send, d_opp)

    def to_opposite(group):
        buf, recv, sib, send, opp = group
        shard = buf.at[z, core, hi]
        return remote(shard, shard, opp.at[0], recv.at[z, hi], opposite)

    def to_line(group, zz, h, way):
        buf, recv, sib, send, opp = group
        shard = buf.at[zz, core, h]
        return remote(shard, shard, send.at[zz, h, way], recv.at[zz, h], (up, down)[way])

    def to_sibling(group, zz, h):
        buf, recv, sib, send, opp = group
        shard = buf.at[zz, core, h]
        return remote(shard, shard, send.at[zz, h, 2], sib.at[zz, h], sibling)

    def await_shard(group, zz, h):
        buf, recv, sib, send, opp = group
        shard = buf.at[zz, core, h]
        remote(shard, shard, send.at[zz, h, 0], recv.at[zz, h], up).wait_recv()

    def await_sibling(group, zz):
        buf, recv, sib, send, opp = group
        for h in range(HI):
            shard = buf.at[zz, 1 - core, h]
            remote(shard, shard, send.at[zz, h, 2], sib.at[zz, h], sibling).wait_recv()

    def ring(group, c, far, act, arrive):
        zz = chunk_z(c)
        h = 1 - hi if far else hi
        way = (c + 1) % 2
        if arrive:
            await_shard(group, zz, h)
        if c < 5 or (c < 7 and way == far):
            act(to_line(group, zz, h, way))

        act(to_sibling(group, zz, h))

    def start(copy):
        copy.start()

    def finish(copy):
        copy.wait_send()

    def chunk_z(t):
        if isinstance(t, int):
            return lax.rem(z + (Z - (t + 1) // 2 if t % 2 else t // 2), Z)
        return lax.rem(z + jnp.where(lax.rem(t, 2) == 1, Z - (t + 1) // 2, t // 2), Z)

    def products(t, lanes):
        zz = chunk_z(t)
        shards = CORE * HI
        lhs = cols[zz].reshape(shards * picks, cols.shape[-1])
        step = 256
        for first in range(lanes.start, lanes.stop, step):
            res = lax.dot_general(
                lhs, x_ref[pl.ds(first, step), :], (((1,), (1,)), ((), ())),
                preferred_element_type=F32,
            )
            for kk in range(LO * YS):
                for g in range(shards):
                    part[t * (LO * YS) + kk, pl.ds(g * 8, 8), pl.ds(first, step)] = res[
                        g * picks + kk * 8 : g * picks + kk * 8 + 8
                    ]

    def part_y(t):
        await_sibling(a_set, chunk_z(t))
        products(t, y_lanes)
        for way in range(2):
            beside = (y_next, y_last)[way]
            blocks = [Rows(part, at(t, lx, y_far), way * HALF, y_lanes) for lx in range(LO)]
            blocks += [Rows(part, at(t, lx, beside), (1 - way) * HALF, y_lanes) for lx in range(LO)]
            encode(blocks, n_out.at[t, way])
            n_copy(t, way).start()

    def part_x(t):
        products(t, x_lanes)
        blocks = []
        for yy in range(YS):
            for first in (0, HALF):
                blocks.append(Rows(part, at(t, xo, yy), first, x_lanes))
        encode(blocks, x_out.at[t])
        x_copy(t).start()

    def n_copy(t, way):
        return remote(
            n_out.at[t, way], n_in.at[t, way], n_send.at[t, way], n_recv.at[t, way], (right, left)[way]
        )

    def p_copy(t, way):
        return remote(
            p_out.at[t, way], p_in.at[t, way], p_send.at[t, way], p_recv.at[t, way], (right, left)[way]
        )

    def w_copy(t):
        return remote(w_out.at[t], w_in.at[t], w_send.at[t], w_recv.at[t], partner)

    def x_copy(t):
        return remote(x_out.at[t], x_in.at[t], x_send.at[t], x_recv.at[t], partner)

    def y_copy(t, way):
        return remote(
            y_out.at[t, way], y_in.at[t, way], y_send.at[t, way], y_recv.at[t, way], (right, left)[way]
        )

    def m_copy(t, way):
        return remote(
            m_out.at[t, way], m_in.at[t, way], m_send.at[t, way], m_recv.at[t, way], (right, left)[way]
        )

    def c_copy(t, block, lane, target):
        spot = scr.at[t, block]
        return remote(spot, spot, c_send.at[t, lane], c_recv.at[t, block], target)

    def at(t, lx, yy):
        return t * (LO * YS) + occ_at(lx, yy)

    def add(block, first, lanes, message, tile, scale):
        for lane in lanes:
            spot = (block, pl.ds(first, HALF), pl.ds(lane, LANE))
            part[spot] = part[spot] + decode(message, tile, scale)
            tile += 1

    def pair_sum(t):
        x_copy(t).wait_recv()
        message = x_in.at[t]
        scale = unit(message, YS * 2 * x_tiles)
        for yy in range(YS):
            for half in range(2):
                add(at(t, lo, yy), half * HALF, x_lanes, message, (yy * 2 + half) * x_tiles, scale)
        for way in range(2):
            beside = (y_next, y_last)[way]
            encode(
                [
                    Rows(part, at(t, lo, y_far), way * HALF, x_lanes),
                    Rows(part, at(t, lo, beside), (1 - way) * HALF, x_lanes),
                ],
                y_out.at[t, way],
            )
            y_copy(t, way).start()

    def pass_on(t):
        for way in range(2):
            beside = (y_next, y_last)[way]
            y_copy(t, way).wait_recv()
            message = y_in.at[t, way]
            add(at(t, lo, beside), way * HALF, x_lanes, message, 0, unit(message, 2 * x_tiles))
            encode([Rows(part, at(t, lo, beside), way * HALF, x_lanes)], m_out.at[t, way])
            m_copy(t, way).start()

    def pass_on_y(t):
        for way in range(2):
            beside = (y_next, y_last)[way]
            n_copy(t, way).wait_recv()
            message = n_in.at[t, way]
            scale = unit(message, 2 * LO * y_tiles)
            for lx in range(LO):
                add(at(t, lx, beside), way * HALF, y_lanes, message, lx * y_tiles, scale)
            encode(
                [Rows(part, at(t, lx, beside), way * HALF, y_lanes) for lx in range(LO)], p_out.at[t, way]
            )
            p_copy(t, way).start()

    def sum_y(t):
        for way in range(2):
            p_copy(t, way).wait_recv()
        for half in range(2):
            near, far = n_in.at[t, 1 - half], p_in.at[t, half]
            near_scale, far_scale = unit(near, 2 * LO * y_tiles), unit(far, LO * y_tiles)
            for lx in range(LO):
                add(at(t, lx, y), half * HALF, y_lanes, near, (LO + lx) * y_tiles, near_scale)
                add(at(t, lx, y), half * HALF, y_lanes, far, lx * y_tiles, far_scale)
        encode([Rows(part, at(t, xo, y), half * HALF, y_lanes) for half in range(2)], w_out.at[t])
        w_copy(t).start()

    def panel(t):
        zz = chunk_z(t)
        for way in range(2):
            m_copy(t, way).wait_recv()
        w_copy(t).wait_recv()
        if t == 0:
            prev_copy.wait()
        other = w_in.at[t]
        other_scale = unit(other, 2 * y_tiles)
        for half in range(2):
            near, far = y_in.at[t, 1 - half], m_in.at[t, half]
            near_scale, far_scale = unit(near, 2 * x_tiles), unit(far, x_tiles)
            for lane in range(0, width, LANE):
                total = part[at(t, lo, y), pl.ds(half * HALF, HALF), pl.ds(lane, LANE)]
                tile = lane // LANE
                if tile < x_tiles:
                    total = total + decode(near, x_tiles + tile, near_scale)
                    total = total + decode(far, tile, far_scale)
                else:
                    total = total + decode(other, half * y_tiles + tile - x_tiles, other_scale)
                kept = []
                for h in range(HI):
                    row = pl.multiple_of(h * (Z * CORE * 8) + zz * (CORE * 8) + half * 8, 8)
                    value = prev_ref[pl.ds(row, 8), pl.ds(lane, LANE)] - total[h * 8 : h * 8 + 8]
                    out_ref[pl.ds(row, 8), pl.ds(lane, LANE)] = value
                    kept.append(value)
                scr[t, k, pl.ds(half * HALF, HALF), pl.ds(lane, LANE)] = jnp.concatenate(
                    kept, axis=0
                ).astype(BF16)
        c_copy(t, k, 0, partner).start()
        c_copy(t, k, 1, right).start()
        c_copy(t, k, 2, left).start()

    def await_block(t, block):
        c_copy(t, block, 0, partner).wait_recv()

    def spread_partner(t):
        block = occ_at(xo, y)
        await_block(t, block)
        c_copy(t, block, 3, right).start()
        c_copy(t, block, 4, left).start()

    def spread_right(t):
        block = occ_at(lo, y_last)
        await_block(t, block)
        c_copy(t, block, 5, right).start()

    def spread_left(t):
        block = occ_at(xo, y_next)
        await_block(t, block)
        c_copy(t, block, 6, left).start()

    def energy(t, quarter):
        zz = chunk_z(t)
        if quarter == 0:
            for block in (occ_at(xo, y_last), occ_at(lo, y_next), occ_at(lo, y_far), occ_at(xo, y_far)):
                await_block(t, block)
            await_sibling(d_set, zz)
        lhs = scr[t].reshape(LO * YS * 2 * HALF, width)
        step = s_ref.shape[1] // 4
        lanes = pl.ds(quarter * step, step)
        applied = jnp.dot(lhs, s_ref[:, lanes], preferred_element_type=F32)
        total = acc[:, lanes]
        for g in range(CORE * HI):
            rows = slab[zz, g // HI, g % HI, :, lanes].astype(F32)
            for kk in range(LO * YS):
                spot = kk * 2 * HALF + g * 8
                total = total + applied[spot : spot + 8] * rows[kk * 8 : kk * 8 + 8]
        acc[:, lanes] = total

    start(to_opposite(a_set))
    start(to_line(a_set, z, hi, 0))
    start(to_line(a_set, z, hi, 1))
    start(to_sibling(a_set, z, hi))

    acc[...] = jnp.zeros_like(acc)

    def to_diagonal():
        return remote(slab.at[z, core, hi], relayed, r_send.at[0], r_recv.at[0], diagonal)

    def relay_on():
        return remote(relayed, slab.at[z, core, 1 - hi], d_opp.at[0], d_recv.at[z, 1 - hi], partner)

    def prepare_states(t):
        states, orbitals = s3_ref.shape[1:]
        depth = wide.shape[0] // states
        s3_copy.wait()

        def spread_states(n, carry):
            at_row = pl.multiple_of(n * depth, depth)
            for lane in range(0, orbitals, LANE):
                raw = s3_ref[pl.ds(at_row, depth), :, pl.ds(lane, LANE)].astype(F32)
                wide[...] = raw.reshape(depth * states, LANE)
                for state in range(states):
                    s_ref[pl.ds(at_row, depth), pl.ds(state * orbitals + lane, LANE)] = wide[
                        pl.ds(state, depth, stride=states), :
                    ].astype(BF16)
            return carry

        lax.fori_loop(0, s3_ref.shape[0] // depth, spread_states, 0)
        slab[z, core, hi] = jnp.dot(chosen, s_ref[...], preferred_element_type=F32).astype(BF16)
        start(to_diagonal())

    def relay(t):
        to_diagonal().wait_recv()
        start(relay_on())

    def first_far(group):
        await_shard(group, z, 1 - hi)
        start(to_sibling(group, z, 1 - hi))
        start(to_line(group, z, 1 - hi, 0))
        start(to_line(group, z, 1 - hi, 1))

    def first_own(t):
        start(to_sibling(d_set, z, hi))
        start(to_line(d_set, z, hi, 0))
        start(to_line(d_set, z, hi, 1))

    stages = {
        RELAY: relay,
        A_OPP: lambda t: first_far(a_set),
        D_OWN: first_own,
        D_OPP: lambda t: first_far(d_set),
        A_RING: lambda t: ring(a_set, t, 0, start, True),
        A_RING2: lambda t: ring(a_set, t, 1, start, True),
        D_RING: lambda t: ring(d_set, t, 0, start, True),
        D_RING2: lambda t: ring(d_set, t, 1, start, True),
        D_PREP: prepare_states,
        PART_Y: part_y,
        PART_X: part_x,
        SUM: pair_sum,
        PASS: pass_on,
        PASS_Y: pass_on_y,
        SUM_Y: sum_y,
        PANEL: panel,
        NEAR: spread_partner,
        FAR_R: spread_right,
        FAR_L: spread_left,
        PAIRS: energy,
    }

    for stage, *spot in ORDER:
        stages[stage](*spot)

    pairs = jnp.sum(acc[...], axis=0, keepdims=True)
    mine = hi * CORE + core
    orbitals = orb_ref.shape[1]
    for n in range(state_idx.shape[0]):
        gap = mo_ref[state_idx[n]] - orb_ref[...]
        factor = gap / (gap * gap + 0.25)
        value = jnp.sum(factor * pairs[:, n * orbitals : (n + 1) * orbitals], axis=1, keepdims=True)
        sg_chip[mine, pl.ds(n, 1), :] = jnp.broadcast_to(value, (1, LANE))

    def chip_copy(n, target):
        spot = sg_chip.at[mine]
        return remote(spot, spot, g_send.at[n], g_recv.at[mine], target)

    chip = [
        (sibling, hi * CORE + 1 - core),
        (opposite, (1 - hi) * CORE + core),
        (across, (1 - hi) * CORE + 1 - core),
    ]
    for n, (target, slot) in enumerate(chip):
        chip_copy(n, target).start()
    for n, (target, slot) in enumerate(chip):
        spot = sg_chip.at[slot]
        remote(spot, spot, g_send.at[n], g_recv.at[slot], target).wait_recv()
    sg_line[z] = (sg_chip[0] + sg_chip[1]) + (sg_chip[2] + sg_chip[3])

    def line_copy(n, target):
        spot = sg_line.at[z]
        return remote(spot, spot, l_send.at[n], l_recv.at[z], target)

    for n, target in enumerate(line):
        line_copy(n, target).start()
    for n, target in enumerate(line):
        slot = lax.rem(z + 1 + n, Z)
        spot = sg_line.at[slot]
        remote(spot, spot, l_send.at[n], l_recv.at[slot], target).wait_recv()
    total = sg_line[0]
    for n in range(1, Z):
        total = total + sg_line[n]
    diag = lax.broadcasted_iota(jnp.int32, total.shape, 0) == lax.broadcasted_iota(jnp.int32, total.shape, 1)
    sig_ref[...] = jnp.sum(jnp.where(diag, total, 0.0), axis=0, keepdims=True)[:, : sig_ref.shape[1]]

    for n, (target, slot) in enumerate(chip):
        chip_copy(n, target).wait_send()
    for n, target in enumerate(line):
        line_copy(n, target).wait_send()
    finish(to_opposite(a_set))
    finish(to_diagonal())
    finish(relay_on())
    for group in (a_set, d_set):
        for h in range(HI):
            finish(to_line(group, z, h, 0))
            finish(to_line(group, z, h, 1))
            finish(to_sibling(group, z, h))

        for c in range(1, CHUNKS):
            ring(group, c, 0, finish, False)
            ring(group, c, 1, finish, False)

    def drain(t, carry):
        x_copy(t).wait_send()
        for way in range(2):
            y_copy(t, way).wait_send()
            m_copy(t, way).wait_send()
            n_copy(t, way).wait_send()
            p_copy(t, way).wait_send()
        w_copy(t).wait_send()
        for lane in range(7):
            c_copy(t, k, lane, partner).wait_send()
        return carry

    lax.fori_loop(0, CHUNKS, drain, 0)


def local(
    three_index,
    polar_prev,
    states,
    mo_energy,
    vir_energy,
    orbital_energy,
    occ_index,
    state_index,
    slab_rows,
):
    ri_count = lax.axis_size("ri")
    occ_count = lax.axis_size("occ")
    assert (ri_count, occ_count) == (HI * Z * CORE, LO * YS)
    p_dev = three_index.shape[0]
    col_block = polar_prev.shape[0]
    picks = slab_rows.shape[0] // ri_count
    ns_dev, orbitals = states.shape[1:]
    flat = three_index.reshape(p_dev, -1)
    pairs = flat.shape[1]
    spread = ns_dev * orbitals
    y_tiles = Y_FIRST
    x_tiles = p_dev // LANE - Y_FIRST

    def message(count, *lead):
        return pltpu.VMEM((CHUNKS, *lead, count + 1, HALF, LANE), jnp.int16)

    vmem = pl.BlockSpec(memory_space=pltpu.VMEM)
    hbm = pl.BlockSpec(memory_space=pl.ANY)
    smem = pl.BlockSpec(memory_space=pltpu.SMEM)
    dma = pltpu.SemaphoreType.DMA
    ring_sems = [dma((Z, HI)), dma((Z, HI)), dma((Z, HI, 3)), dma((1,))]
    panel_out, sig = pl.pallas_call(
        kernel,
        out_shape=(
            jax.ShapeDtypeStruct((col_block, p_dev), F32),
            jax.ShapeDtypeStruct((1, ns_dev), F32),
        ),
        in_specs=[vmem, hbm, hbm, vmem, vmem] + [smem] * 4,
        out_specs=(vmem, vmem),
        scratch_shapes=[
            pltpu.VMEM((Z, CORE, HI, picks, pairs), BF16),
            pltpu.VMEM((Z, CORE, HI, picks, spread), BF16),
            pltpu.VMEM((CHUNKS * occ_count, 2 * HALF, p_dev), F32),
            message(YS * 2 * x_tiles), message(YS * 2 * x_tiles),
            message(2 * x_tiles, 2), message(2 * x_tiles, 2),
            message(x_tiles, 2), message(x_tiles, 2),
            message(2 * LO * y_tiles, 2), message(2 * LO * y_tiles, 2),
            message(LO * y_tiles, 2), message(LO * y_tiles, 2),
            message(2 * y_tiles), message(2 * y_tiles),
            pltpu.VMEM((CHUNKS, occ_count, 2 * HALF, p_dev), BF16),
            pltpu.VMEM((8, spread), F32),
            pltpu.VMEM((HI * CORE, 8, LANE), F32),
            pltpu.VMEM((Z, 8, LANE), F32),
            pltpu.VMEM((p_dev, spread), BF16),
            pltpu.VMEM((LANE * ns_dev, LANE), F32),
            pltpu.VMEM((picks, spread), BF16),
            pltpu.VMEM((p_dev, ns_dev, orbitals), BF16),
            pltpu.VMEM((col_block, p_dev), F32),
            *ring_sems,
            *ring_sems,
            dma((CHUNKS,)), dma((CHUNKS,)),
            dma((CHUNKS, 2)), dma((CHUNKS, 2)),
            dma((CHUNKS, 2)), dma((CHUNKS, 2)),
            dma((CHUNKS, 2)), dma((CHUNKS, 2)),
            dma((CHUNKS, 2)), dma((CHUNKS, 2)),
            dma((CHUNKS,)), dma((CHUNKS,)),
            dma((CHUNKS, 7)), dma((CHUNKS, occ_count)),
            dma((3,)), dma((HI * CORE,)),
            dma((Z - 1,)), dma((Z,)),
            dma((1,)), dma((1,)), dma((2,)),
        ],
        compiler_params=pltpu.CompilerParams(
            collective_id=0, has_side_effects=True, vmem_limit_bytes=60 * 2**20
        ),
        cost_estimate=pl.CostEstimate(
            flops=13 * 10**9, bytes_accessed=9 * 2**20, transcendentals=0
        ),
    )(
        flat, states, polar_prev,
        vir_energy.reshape(1, -1), orbital_energy.reshape(1, -1),
        mo_energy, occ_index, state_index, slab_rows,
    )
    return (panel_out, sig.reshape(ns_dev))


def solution(mesh):
    in_specs = (
        P("ri", "occ", None),
        P("occ", "ri"),
        P("ri", "occ", None),
        P(),
        P(),
        P(),
        P("occ"),
        P("occ"),
        P(),
    )
    out_specs = (P("occ", "ri"), P("occ"))
    return jax.shard_map(local, mesh=mesh, in_specs=in_specs, out_specs=out_specs, check_vma=False)
```

```python
import jax
import jax.numpy as jnp
from jax import lax
from jax.experimental import pallas as pl
from jax.experimental.pallas import tpu as pltpu
from jax.sharding import PartitionSpec as P

HI, Z, CORE, LO, YS = 2, 8, 2, 2, 4
CHUNKS = Z
LANE = 128
HALF = 16
Y_FIRST = 4

(
    RELAY, A_OPP, D_PREP, D_OWN, D_OPP, A_RING, A_RING2, D_RING, D_RING2, PART_Y, PART_X, SUM, PASS, PASS_Y,
    SUM_Y, PANEL, NEAR, FAR_R, FAR_L, PAIRS,
) = range(20)
ORDER = (
    (D_PREP, 0), (A_RING, 1), (A_RING, 2), (A_OPP, 0), (PART_Y, 0), (PART_X, 0), (PASS_Y, 0), (A_RING, 3),
    (A_RING, 4), (A_RING2, 1), (A_RING2, 2), (RELAY, 0), (SUM, 0), (SUM_Y, 0), (PART_Y, 1), (PART_X, 1),
    (PASS, 0), (PART_Y, 2), (PART_X, 2), (A_RING, 5), (A_RING, 6), (A_RING2, 3), (A_RING2, 4), (PANEL, 0),
    (PASS_Y, 1), (PASS_Y, 2), (PART_Y, 3), (PART_X, 3), (D_OWN, 0), (A_RING2, 6), (SUM_Y, 1), (FAR_R, 0),
    (PART_Y, 4), (PART_X, 4), (SUM_Y, 2), (D_OPP, 0), (PASS_Y, 3), (A_RING, 7), (A_RING2, 5), (NEAR, 0),
    (SUM, 1), (PART_Y, 5), (PART_X, 5), (FAR_L, 0), (PASS_Y, 4), (SUM_Y, 3), (PART_Y, 6), (SUM, 2),
    (PART_X, 6), (PASS, 1), (A_RING2, 7), (PART_Y, 7), (PASS_Y, 5), (PART_X, 7), (PANEL, 1), (D_RING, 1),
    (PASS, 2), (SUM_Y, 4), (SUM, 3), (D_RING2, 1), (PAIRS, 0, 0), (D_RING, 2), (PASS_Y, 6), (PAIRS, 0, 1),
    (SUM, 4), (D_RING2, 2), (PAIRS, 0, 2), (PAIRS, 0, 3), (SUM_Y, 5), (PANEL, 2), (PASS_Y, 7), (PASS, 3),
    (FAR_R, 1), (SUM_Y, 6), (PASS, 4), (SUM, 5), (FAR_R, 2), (NEAR, 1), (PANEL, 3), (SUM_Y, 7), (PANEL, 4),
    (SUM, 6), (D_RING, 3), (D_RING2, 3), (NEAR, 2), (D_RING, 4), (D_RING2, 4), (FAR_L, 1), (PASS, 5),
    (SUM, 7), (NEAR, 3), (NEAR, 4), (PASS, 6), (PANEL, 5), (FAR_R, 3), (FAR_L, 2), (FAR_R, 4), (NEAR, 5),
    (PASS, 7), (PAIRS, 1, 0), (PANEL, 6), (D_RING, 5), (PAIRS, 1, 1), (PAIRS, 1, 2), (FAR_L, 3), (D_RING2, 5),
    (D_RING, 6), (FAR_L, 4), (PAIRS, 1, 3), (D_RING2, 6), (NEAR, 6), (PANEL, 7), (PAIRS, 2, 0), (PAIRS, 2, 1),
    (PAIRS, 2, 2), (NEAR, 7), (D_RING, 7), (FAR_R, 5), (PAIRS, 2, 3), (FAR_L, 5), (D_RING2, 7), (FAR_R, 6),
    (PAIRS, 3, 0), (PAIRS, 3, 1), (PAIRS, 3, 2), (PAIRS, 3, 3), (FAR_L, 6), (PAIRS, 4, 0), (FAR_R, 7),
    (PAIRS, 4, 1), (PAIRS, 4, 2), (PAIRS, 4, 3), (FAR_L, 7), (PAIRS, 5, 0), (PAIRS, 5, 1), (PAIRS, 5, 2),
    (PAIRS, 5, 3), (PAIRS, 6, 0), (PAIRS, 6, 1), (PAIRS, 6, 2), (PAIRS, 6, 3), (PAIRS, 7, 0), (PAIRS, 7, 1),
    (PAIRS, 7, 2), (PAIRS, 7, 3),
)

MESH = pl.DeviceIdType.MESH
F32 = jnp.float32
BF16 = jnp.bfloat16


def remote(src, dst, send_sem, recv_sem, target):
    return pltpu.make_async_remote_copy(
        src_ref=src, dst_ref=dst, send_sem=send_sem, recv_sem=recv_sem,
        device_id=target, device_id_type=MESH,
    )


def tile_scale(peak):
    return jnp.floor(jnp.log(jnp.maximum(peak, 1e-20) * 1.001) * 1.4426950408889634) + 1.0


def encode(blocks, message):
    peak = None
    for load in blocks:
        for lane in load.lanes:
            high = jnp.abs(load(lane))
            peak = high if peak is None else jnp.maximum(peak, high)
    exponent = tile_scale(peak)
    inverse = jnp.exp2(15.0 - exponent)
    at = 0
    for load in blocks:
        for lane in load.lanes:
            message[at] = (load(lane) * inverse).astype(jnp.int32).astype(jnp.int16)
            at += 1
    message[at] = exponent.astype(jnp.int32).astype(jnp.int16)


def unit(message, last):
    return jnp.exp2(message[last].astype(jnp.int32).astype(F32) - 15.0)


def decode(message, at, scale):
    return message[at].astype(jnp.int32).astype(F32) * scale


class Rows:
    def __init__(self, ref, block, first, lanes):
        self.ref, self.block, self.first, self.lanes = ref, block, first, lanes

    def __call__(self, lane):
        return self.ref[self.block, pl.ds(self.first, HALF), pl.ds(lane, LANE)]


def kernel(
    x3_ref, s3_hbm, prev_hbm, vir_ref, orb_ref, mo_ref, occ_idx, state_idx, slab_rows,
    out_ref, sig_ref,
    cols, slab, part, x_out, x_in, y_out, y_in, m_out, m_in, n_out, n_in, p_out, p_in, w_out, w_in,
    scr, acc, sg_chip, sg_line, s_ref, wide, relayed, s3_ref, prev_ref, x_ref, few,
    a_recv, a_sib, a_send, a_opp, d_recv, d_sib, d_send, d_opp,
    x_send, x_recv, y_send, y_recv, m_send, m_recv, n_send, n_recv, p_send, p_recv, w_send, w_recv,
    c_send, c_recv, g_send, g_recv, l_send, l_recv, r_send, r_recv, load,
):
    width = prev_ref.shape[1]
    x_lanes = range(0, width - Y_FIRST * LANE, LANE)
    y_lanes = range(width - Y_FIRST * LANE, width, LANE)
    x_tiles, y_tiles = len(x_lanes), len(y_lanes)
    ri, k = lax.axis_index("ri"), lax.axis_index("occ")
    core = lax.rem(ri, CORE)
    z = lax.rem(ri // CORE, Z)
    hi = ri // (CORE * Z)
    y = lax.rem(k, YS)
    lo = k // YS
    xo = 1 - lo

    def ri_at(h, zz, c):
        return (h * Z + zz) * CORE + c

    def occ_at(x, yy):
        return x * YS + yy

    up = (ri_at(hi, lax.rem(z + 1, Z), core), k)
    down = (ri_at(hi, lax.rem(z + Z - 1, Z), core), k)
    sibling = (ri_at(hi, z, 1 - core), k)
    opposite = (ri_at(1 - hi, z, core), k)
    across = (ri_at(1 - hi, z, 1 - core), k)
    partner = (ri, occ_at(xo, y))
    diagonal = (ri_at(1 - hi, z, core), occ_at(xo, y))
    y_next, y_last, y_far = lax.rem(y + 1, YS), lax.rem(y + YS - 1, YS), lax.rem(y + 2, YS)
    right, left = (ri, occ_at(lo, y_next)), (ri, occ_at(lo, y_last))
    line = [(ri_at(hi, lax.rem(z + s, Z), core), k) for s in range(1, Z)]

    s3_copy = pltpu.make_async_copy(s3_hbm, s3_ref, load.at[0])
    prev_copy = pltpu.make_async_copy(prev_hbm, prev_ref, load.at[1])
    barrier = pltpu.get_barrier_semaphore()
    friends = [sibling, opposite, across, partner, diagonal, right, left] + line
    for friend in friends:
        pl.semaphore_signal(barrier, inc=1, device_id=friend, device_id_type=MESH)

    s3_copy.start()
    prev_copy.start()

    per_sub = prev_ref.shape[0] // (HI * Z * CORE)
    picks = LO * YS * per_sub
    pairs_in, virtual = x3_ref.shape[1:]
    local_rows = [
        lax.rem(slab_rows[kk * prev_ref.shape[0] + ri * per_sub + s], x3_ref.shape[0])
        for kk in range(LO * YS)
        for s in range(per_sub)
    ]
    few_rows = few.reshape(virtual // LANE, picks * 8, LANE)
    for j, row in enumerate(local_rows):
        raw = x3_ref[row].astype(F32)
        for lane in range(0, virtual, LANE):
            few[lane // LANE, j, pl.ds(0, pairs_in), :] = raw[:, lane : lane + LANE]
    for i in range(pairs_in):
        gap = vir_ref[...] - mo_ref[occ_idx[i]]
        weight = 4.0 * gap / (gap * gap + 0.25)
        for lane in range(0, virtual, LANE):
            picked = few_rows[lane // LANE, pl.ds(i, picks, stride=8), :]
            cols[z, core, hi, :, pl.ds(i * virtual + lane, LANE)] = (
                picked * weight[:, lane : lane + LANE]
            ).astype(BF16)

    pl.semaphore_wait(barrier, len(friends))

    a_set = (cols, a_recv, a_sib, a_send, a_opp)
    d_set = (slab, d_recv, d_sib, d_send, d_opp)

    def to_opposite(group):
        buf, recv, sib, send, opp = group
        shard = buf.at[z, core, hi]
        return remote(shard, shard, opp.at[0], recv.at[z, hi], opposite)

    def to_line(group, zz, h, way):
        buf, recv, sib, send, opp = group
        shard = buf.at[zz, core, h]
        return remote(shard, shard, send.at[zz, h, way], recv.at[zz, h], (up, down)[way])

    def to_sibling(group, zz, h):
        buf, recv, sib, send, opp = group
        shard = buf.at[zz, core, h]
        return remote(shard, shard, send.at[zz, h, 2], sib.at[zz, h], sibling)

    def await_shard(group, zz, h):
        buf, recv, sib, send, opp = group
        shard = buf.at[zz, core, h]
        remote(shard, shard, send.at[zz, h, 0], recv.at[zz, h], up).wait_recv()

    def await_sibling(group, zz):
        buf, recv, sib, send, opp = group
        for h in range(HI):
            shard = buf.at[zz, 1 - core, h]
            remote(shard, shard, send.at[zz, h, 2], sib.at[zz, h], sibling).wait_recv()

    def ring(group, c, far, act, arrive):
        zz = chunk_z(c)
        h = 1 - hi if far else hi
        way = (c + 1) % 2
        if arrive:
            await_shard(group, zz, h)
        if c < 5 or (c < 7 and way == far):
            act(to_line(group, zz, h, way))

        act(to_sibling(group, zz, h))

    def start(copy):
        copy.start()

    def finish(copy):
        copy.wait_send()

    def chunk_z(t):
        if isinstance(t, int):
            return lax.rem(z + (Z - (t + 1) // 2 if t % 2 else t // 2), Z)
        return lax.rem(z + jnp.where(lax.rem(t, 2) == 1, Z - (t + 1) // 2, t // 2), Z)

    def products(t, lanes):
        zz = chunk_z(t)
        shards = CORE * HI
        lhs = cols[zz].reshape(shards * picks, cols.shape[-1])
        step = 256
        for first in range(lanes.start, lanes.stop, step):
            res = lax.dot_general(
                lhs, x_ref[pl.ds(first, step), :], (((1,), (1,)), ((), ())),
                preferred_element_type=F32,
            )
            for kk in range(LO * YS):
                for g in range(shards):
                    part[t * (LO * YS) + kk, pl.ds(g * 8, 8), pl.ds(first, step)] = res[
                        g * picks + kk * 8 : g * picks + kk * 8 + 8
                    ]

    def part_y(t):
        await_sibling(a_set, chunk_z(t))
        products(t, y_lanes)
        for way in range(2):
            beside = (y_next, y_last)[way]
            blocks = [Rows(part, at(t, lx, y_far), way * HALF, y_lanes) for lx in range(LO)]
            blocks += [Rows(part, at(t, lx, beside), (1 - way) * HALF, y_lanes) for lx in range(LO)]
            encode(blocks, n_out.at[t, way])
            n_copy(t, way).start()

    def part_x(t):
        products(t, x_lanes)
        blocks = []
        for yy in range(YS):
            for first in (0, HALF):
                blocks.append(Rows(part, at(t, xo, yy), first, x_lanes))
        encode(blocks, x_out.at[t])
        x_copy(t).start()

    def n_copy(t, way):
        return remote(
            n_out.at[t, way], n_in.at[t, way], n_send.at[t, way], n_recv.at[t, way], (right, left)[way]
        )

    def p_copy(t, way):
        return remote(
            p_out.at[t, way], p_in.at[t, way], p_send.at[t, way], p_recv.at[t, way], (right, left)[way]
        )

    def w_copy(t):
        return remote(w_out.at[t], w_in.at[t], w_send.at[t], w_recv.at[t], partner)

    def x_copy(t):
        return remote(x_out.at[t], x_in.at[t], x_send.at[t], x_recv.at[t], partner)

    def y_copy(t, way):
        return remote(
            y_out.at[t, way], y_in.at[t, way], y_send.at[t, way], y_recv.at[t, way], (right, left)[way]
        )

    def m_copy(t, way):
        return remote(
            m_out.at[t, way], m_in.at[t, way], m_send.at[t, way], m_recv.at[t, way], (right, left)[way]
        )

    def c_copy(t, block, lane, target):
        spot = scr.at[t, block]
        return remote(spot, spot, c_send.at[t, lane], c_recv.at[t, block], target)

    def at(t, lx, yy):
        return t * (LO * YS) + occ_at(lx, yy)

    def add(block, first, lanes, message, tile, scale):
        for lane in lanes:
            spot = (block, pl.ds(first, HALF), pl.ds(lane, LANE))
            part[spot] = part[spot] + decode(message, tile, scale)
            tile += 1

    def pair_sum(t):
        x_copy(t).wait_recv()
        message = x_in.at[t]
        scale = unit(message, YS * 2 * x_tiles)
        for yy in range(YS):
            for half in range(2):
                add(at(t, lo, yy), half * HALF, x_lanes, message, (yy * 2 + half) * x_tiles, scale)
        for way in range(2):
            beside = (y_next, y_last)[way]
            encode(
                [
                    Rows(part, at(t, lo, y_far), way * HALF, x_lanes),
                    Rows(part, at(t, lo, beside), (1 - way) * HALF, x_lanes),
                ],
                y_out.at[t, way],
            )
            y_copy(t, way).start()

    def pass_on(t):
        for way in range(2):
            beside = (y_next, y_last)[way]
            y_copy(t, way).wait_recv()
            message = y_in.at[t, way]
            add(at(t, lo, beside), way * HALF, x_lanes, message, 0, unit(message, 2 * x_tiles))
            encode([Rows(part, at(t, lo, beside), way * HALF, x_lanes)], m_out.at[t, way])
            m_copy(t, way).start()

    def pass_on_y(t):
        for way in range(2):
            beside = (y_next, y_last)[way]
            n_copy(t, way).wait_recv()
            message = n_in.at[t, way]
            scale = unit(message, 2 * LO * y_tiles)
            for lx in range(LO):
                add(at(t, lx, beside), way * HALF, y_lanes, message, lx * y_tiles, scale)
            encode(
                [Rows(part, at(t, lx, beside), way * HALF, y_lanes) for lx in range(LO)], p_out.at[t, way]
            )
            p_copy(t, way).start()

    def sum_y(t):
        for way in range(2):
            p_copy(t, way).wait_recv()
        for half in range(2):
            near, far = n_in.at[t, 1 - half], p_in.at[t, half]
            near_scale, far_scale = unit(near, 2 * LO * y_tiles), unit(far, LO * y_tiles)
            for lx in range(LO):
                add(at(t, lx, y), half * HALF, y_lanes, near, (LO + lx) * y_tiles, near_scale)
                add(at(t, lx, y), half * HALF, y_lanes, far, lx * y_tiles, far_scale)
        encode([Rows(part, at(t, xo, y), half * HALF, y_lanes) for half in range(2)], w_out.at[t])
        w_copy(t).start()

    def panel(t):
        zz = chunk_z(t)
        for way in range(2):
            m_copy(t, way).wait_recv()
        w_copy(t).wait_recv()
        if t == 0:
            prev_copy.wait()
        other = w_in.at[t]
        other_scale = unit(other, 2 * y_tiles)
        for half in range(2):
            near, far = y_in.at[t, 1 - half], m_in.at[t, half]
            near_scale, far_scale = unit(near, 2 * x_tiles), unit(far, x_tiles)
            for lane in range(0, width, LANE):
                total = part[at(t, lo, y), pl.ds(half * HALF, HALF), pl.ds(lane, LANE)]
                tile = lane // LANE
                if tile < x_tiles:
                    total = total + decode(near, x_tiles + tile, near_scale)
                    total = total + decode(far, tile, far_scale)
                else:
                    total = total + decode(other, half * y_tiles + tile - x_tiles, other_scale)
                kept = []
                for h in range(HI):
                    row = pl.multiple_of(h * (Z * CORE * 8) + zz * (CORE * 8) + half * 8, 8)
                    value = prev_ref[pl.ds(row, 8), pl.ds(lane, LANE)] - total[h * 8 : h * 8 + 8]
                    out_ref[pl.ds(row, 8), pl.ds(lane, LANE)] = value
                    kept.append(value)
                scr[t, k, pl.ds(half * HALF, HALF), pl.ds(lane, LANE)] = jnp.concatenate(
                    kept, axis=0
                ).astype(BF16)
        c_copy(t, k, 0, partner).start()
        c_copy(t, k, 1, right).start()
        c_copy(t, k, 2, left).start()

    def await_block(t, block):
        c_copy(t, block, 0, partner).wait_recv()

    def spread_partner(t):
        block = occ_at(xo, y)
        await_block(t, block)
        c_copy(t, block, 3, right).start()
        c_copy(t, block, 4, left).start()

    def spread_right(t):
        block = occ_at(lo, y_last)
        await_block(t, block)
        c_copy(t, block, 5, right).start()

    def spread_left(t):
        block = occ_at(xo, y_next)
        await_block(t, block)
        c_copy(t, block, 6, left).start()

    def energy(t, quarter):
        zz = chunk_z(t)
        if quarter == 0:
            for block in (occ_at(xo, y_last), occ_at(lo, y_next), occ_at(lo, y_far), occ_at(xo, y_far)):
                await_block(t, block)
            await_sibling(d_set, zz)
        lhs = scr[t].reshape(LO * YS * 2 * HALF, width)
        step = s_ref.shape[1] // 4
        lanes = pl.ds(quarter * step, step)
        applied = jnp.dot(lhs, s_ref[:, lanes], preferred_element_type=F32)
        total = acc[:, lanes]
        for g in range(CORE * HI):
            rows = slab[zz, g // HI, g % HI, :, lanes].astype(F32)
            for kk in range(LO * YS):
                spot = kk * 2 * HALF + g * 8
                total = total + applied[spot : spot + 8] * rows[kk * 8 : kk * 8 + 8]
        acc[:, lanes] = total

    start(to_opposite(a_set))
    start(to_line(a_set, z, hi, 0))
    start(to_line(a_set, z, hi, 1))
    start(to_sibling(a_set, z, hi))

    depth = wide.shape[0] // 8
    wide_rows = wide.reshape(depth, 8, LANE)

    def spread_block(n, carry):
        at_row = pl.multiple_of(n * depth, depth)
        for lane in range(0, virtual, LANE):
            wide_rows[:, pl.ds(0, pairs_in), :] = x3_ref[pl.ds(at_row, depth), :, pl.ds(lane, LANE)].astype(F32)
            for i in range(pairs_in):
                x_ref[pl.ds(at_row, depth), pl.ds(i * virtual + lane, LANE)] = wide[
                    pl.ds(i, depth, stride=8), :
                ].astype(BF16)
        return carry

    lax.fori_loop(0, x3_ref.shape[0] // depth, spread_block, 0)
    groups = []
    for kk in range(LO * YS):
        spot = lax.broadcasted_iota(jnp.int32, (per_sub, LANE), 0)
        rows = jnp.zeros((per_sub, LANE), jnp.int32)
        for s in range(per_sub):
            rows = jnp.where(spot == s, local_rows[kk * per_sub + s], rows)
        groups.append(rows)
    rows = jnp.concatenate(groups, axis=0)
    place = lax.broadcasted_iota(jnp.int32, (picks, LANE), 1)
    chosen = jnp.concatenate(
        [jnp.where(place + lane == rows, 1.0, 0.0) for lane in range(0, x_ref.shape[0], LANE)], axis=1
    ).astype(BF16)
    acc[...] = jnp.zeros_like(acc)

    def to_diagonal():
        return remote(slab.at[z, core, hi], relayed, r_send.at[0], r_recv.at[0], diagonal)

    def relay_on():
        return remote(relayed, slab.at[z, core, 1 - hi], d_opp.at[0], d_recv.at[z, 1 - hi], partner)

    def prepare_states(t):
        states, orbitals = s3_ref.shape[1:]
        assert states == 8
        s3_copy.wait()

        def spread_states(n, carry):
            at_row = pl.multiple_of(n * depth, depth)
            for lane in range(0, orbitals, LANE):
                raw = s3_ref[pl.ds(at_row, depth), :, pl.ds(lane, LANE)].astype(F32)
                wide[...] = raw.reshape(depth * states, LANE)
                for state in range(states):
                    s_ref[pl.ds(at_row, depth), pl.ds(state * orbitals + lane, LANE)] = wide[
                        pl.ds(state, depth, stride=states), :
                    ].astype(BF16)
            return carry

        lax.fori_loop(0, s3_ref.shape[0] // depth, spread_states, 0)
        slab[z, core, hi] = jnp.dot(chosen, s_ref[...], preferred_element_type=F32).astype(BF16)
        start(to_diagonal())

    def relay(t):
        to_diagonal().wait_recv()
        start(relay_on())

    def first_far(group):
        await_shard(group, z, 1 - hi)
        start(to_sibling(group, z, 1 - hi))
        start(to_line(group, z, 1 - hi, 0))
        start(to_line(group, z, 1 - hi, 1))

    def first_own(t):
        start(to_sibling(d_set, z, hi))
        start(to_line(d_set, z, hi, 0))
        start(to_line(d_set, z, hi, 1))

    stages = {
        RELAY: relay,
        A_OPP: lambda t: first_far(a_set),
        D_OWN: first_own,
        D_OPP: lambda t: first_far(d_set),
        A_RING: lambda t: ring(a_set, t, 0, start, True),
        A_RING2: lambda t: ring(a_set, t, 1, start, True),
        D_RING: lambda t: ring(d_set, t, 0, start, True),
        D_RING2: lambda t: ring(d_set, t, 1, start, True),
        D_PREP: prepare_states,
        PART_Y: part_y,
        PART_X: part_x,
        SUM: pair_sum,
        PASS: pass_on,
        PASS_Y: pass_on_y,
        SUM_Y: sum_y,
        PANEL: panel,
        NEAR: spread_partner,
        FAR_R: spread_right,
        FAR_L: spread_left,
        PAIRS: energy,
    }

    for stage, *spot in ORDER:
        stages[stage](*spot)

    pairs = jnp.sum(acc[...], axis=0, keepdims=True)
    mine = hi * CORE + core
    orbitals = orb_ref.shape[1]
    for n in range(state_idx.shape[0]):
        gap = mo_ref[state_idx[n]] - orb_ref[...]
        factor = gap / (gap * gap + 0.25)
        value = jnp.sum(factor * pairs[:, n * orbitals : (n + 1) * orbitals], axis=1, keepdims=True)
        sg_chip[mine, pl.ds(n, 1), :] = jnp.broadcast_to(value, (1, LANE))

    def chip_copy(n, target):
        spot = sg_chip.at[mine]
        return remote(spot, spot, g_send.at[n], g_recv.at[mine], target)

    chip = [
        (sibling, hi * CORE + 1 - core),
        (opposite, (1 - hi) * CORE + core),
        (across, (1 - hi) * CORE + 1 - core),
    ]
    for n, (target, slot) in enumerate(chip):
        chip_copy(n, target).start()
    for n, (target, slot) in enumerate(chip):
        spot = sg_chip.at[slot]
        remote(spot, spot, g_send.at[n], g_recv.at[slot], target).wait_recv()
    sg_line[z] = (sg_chip[0] + sg_chip[1]) + (sg_chip[2] + sg_chip[3])

    def line_copy(n, target):
        spot = sg_line.at[z]
        return remote(spot, spot, l_send.at[n], l_recv.at[z], target)

    for n, target in enumerate(line):
        line_copy(n, target).start()
    for n, target in enumerate(line):
        slot = lax.rem(z + 1 + n, Z)
        spot = sg_line.at[slot]
        remote(spot, spot, l_send.at[n], l_recv.at[slot], target).wait_recv()
    total = sg_line[0]
    for n in range(1, Z):
        total = total + sg_line[n]
    diag = lax.broadcasted_iota(jnp.int32, total.shape, 0) == lax.broadcasted_iota(jnp.int32, total.shape, 1)
    sig_ref[...] = jnp.sum(jnp.where(diag, total, 0.0), axis=0, keepdims=True)[:, : sig_ref.shape[1]]

    for n, (target, slot) in enumerate(chip):
        chip_copy(n, target).wait_send()
    for n, target in enumerate(line):
        line_copy(n, target).wait_send()
    finish(to_opposite(a_set))
    finish(to_diagonal())
    finish(relay_on())
    for group in (a_set, d_set):
        for h in range(HI):
            finish(to_line(group, z, h, 0))
            finish(to_line(group, z, h, 1))
            finish(to_sibling(group, z, h))

        for c in range(1, CHUNKS):
            ring(group, c, 0, finish, False)
            ring(group, c, 1, finish, False)

    def drain(t, carry):
        x_copy(t).wait_send()
        for way in range(2):
            y_copy(t, way).wait_send()
            m_copy(t, way).wait_send()
            n_copy(t, way).wait_send()
            p_copy(t, way).wait_send()
        w_copy(t).wait_send()
        for lane in range(7):
            c_copy(t, k, lane, partner).wait_send()
        return carry

    lax.fori_loop(0, CHUNKS, drain, 0)


def local(
    three_index,
    polar_prev,
    states,
    mo_energy,
    vir_energy,
    orbital_energy,
    occ_index,
    state_index,
    slab_rows,
):
    ri_count = lax.axis_size("ri")
    occ_count = lax.axis_size("occ")
    assert (ri_count, occ_count) == (HI * Z * CORE, LO * YS)
    p_dev = three_index.shape[0]
    col_block = polar_prev.shape[0]
    picks = slab_rows.shape[0] // ri_count
    ns_dev, orbitals = states.shape[1:]
    pairs = three_index.shape[1] * three_index.shape[2]
    spread = ns_dev * orbitals
    y_tiles = Y_FIRST
    x_tiles = p_dev // LANE - Y_FIRST

    def message(count, *lead):
        return pltpu.VMEM((CHUNKS, *lead, count + 1, HALF, LANE), jnp.int16)

    vmem = pl.BlockSpec(memory_space=pltpu.VMEM)
    hbm = pl.BlockSpec(memory_space=pl.ANY)
    smem = pl.BlockSpec(memory_space=pltpu.SMEM)
    dma = pltpu.SemaphoreType.DMA
    ring_sems = [dma((Z, HI)), dma((Z, HI)), dma((Z, HI, 3)), dma((1,))]
    panel_out, sig = pl.pallas_call(
        kernel,
        out_shape=(
            jax.ShapeDtypeStruct((col_block, p_dev), F32),
            jax.ShapeDtypeStruct((1, ns_dev), F32),
        ),
        in_specs=[vmem, hbm, hbm, vmem, vmem] + [smem] * 4,
        out_specs=(vmem, vmem),
        scratch_shapes=[
            pltpu.VMEM((Z, CORE, HI, picks, pairs), BF16),
            pltpu.VMEM((Z, CORE, HI, picks, spread), BF16),
            pltpu.VMEM((CHUNKS * occ_count, 2 * HALF, p_dev), F32),
            message(YS * 2 * x_tiles), message(YS * 2 * x_tiles),
            message(2 * x_tiles, 2), message(2 * x_tiles, 2),
            message(x_tiles, 2), message(x_tiles, 2),
            message(2 * LO * y_tiles, 2), message(2 * LO * y_tiles, 2),
            message(LO * y_tiles, 2), message(LO * y_tiles, 2),
            message(2 * y_tiles), message(2 * y_tiles),
            pltpu.VMEM((CHUNKS, occ_count, 2 * HALF, p_dev), BF16),
            pltpu.VMEM((8, spread), F32),
            pltpu.VMEM((HI * CORE, 8, LANE), F32),
            pltpu.VMEM((Z, 8, LANE), F32),
            pltpu.VMEM((p_dev, spread), BF16),
            pltpu.VMEM((LANE * ns_dev, LANE), F32),
            pltpu.VMEM((picks, spread), BF16),
            pltpu.VMEM((p_dev, ns_dev, orbitals), BF16),
            pltpu.VMEM((col_block, p_dev), F32),
            pltpu.VMEM((p_dev, pairs), BF16),
            pltpu.VMEM((three_index.shape[2] // LANE, picks, 8, LANE), F32),
            *ring_sems,
            *ring_sems,
            dma((CHUNKS,)), dma((CHUNKS,)),
            dma((CHUNKS, 2)), dma((CHUNKS, 2)),
            dma((CHUNKS, 2)), dma((CHUNKS, 2)),
            dma((CHUNKS, 2)), dma((CHUNKS, 2)),
            dma((CHUNKS, 2)), dma((CHUNKS, 2)),
            dma((CHUNKS,)), dma((CHUNKS,)),
            dma((CHUNKS, 7)), dma((CHUNKS, occ_count)),
            dma((3,)), dma((HI * CORE,)),
            dma((Z - 1,)), dma((Z,)),
            dma((1,)), dma((1,)), dma((2,)),
        ],
        compiler_params=pltpu.CompilerParams(
            collective_id=0, has_side_effects=True, vmem_limit_bytes=60 * 2**20
        ),
        cost_estimate=pl.CostEstimate(
            flops=13 * 10**9, bytes_accessed=9 * 2**20, transcendentals=0
        ),
    )(
        three_index, states, polar_prev,
        vir_energy.reshape(1, -1), orbital_energy.reshape(1, -1),
        mo_energy, occ_index, state_index, slab_rows,
    )
    return (panel_out, sig.reshape(ns_dev))


def solution(mesh):
    in_specs = (
        P("ri", "occ", None),
        P("occ", "ri"),
        P("ri", "occ", None),
        P(),
        P(),
        P(),
        P("occ"),
        P("occ"),
        P(),
    )
    out_specs = (P("occ", "ri"), P("occ"))
    return jax.shard_map(local, mesh=mesh, in_specs=in_specs, out_specs=out_specs, check_vma=False)
```

```python
import jax
import jax.numpy as jnp
from jax import lax
from jax.experimental import pallas as pl
from jax.experimental.pallas import tpu as pltpu
from jax.sharding import PartitionSpec as P

HI, Z, CORE, LO, YS = 2, 8, 2, 2, 4
CHUNKS = Z
LANE = 128
HALF = 16
Y_FIRST = 4

(
    RELAY, A_OPP, D_PREP, D_OWN, D_OPP, A_RING, A_RING2, D_RING, D_RING2, PART_Y, PART_X, SUM, PASS, PASS_Y,
    SUM_Y, PANEL, NEAR, FAR_R, FAR_L, PAIRS, X_SPREAD, S_SPREAD,
) = range(22)
ORDER = (
    (X_SPREAD, 4), (X_SPREAD, 5), (X_SPREAD, 6), (X_SPREAD, 7), (X_SPREAD, 0), (X_SPREAD, 1), (X_SPREAD, 2),
    (X_SPREAD, 3), (D_PREP, 0), (A_RING, 1), (A_RING, 2), (A_OPP, 0), (S_SPREAD, 0), (S_SPREAD, 1),
    (S_SPREAD, 2), (PART_Y, 0), (PART_X, 0), (S_SPREAD, 3), (S_SPREAD, 4), (PASS_Y, 0), (RELAY, 0),
    (A_RING2, 1), (A_RING2, 2), (A_RING, 3), (A_RING, 4), (S_SPREAD, 5), (S_SPREAD, 6), (SUM, 0), (SUM_Y, 0),
    (PART_Y, 1), (PART_Y, 2), (PART_X, 1), (PASS, 0), (PART_X, 2), (S_SPREAD, 7), (A_RING2, 3), (A_RING2, 4),
    (A_RING, 5), (A_RING, 6), (D_OWN, 0), (PASS_Y, 1), (PANEL, 0), (PASS_Y, 2), (PART_Y, 3), (PART_Y, 4),
    (D_OPP, 0), (PART_X, 3), (FAR_R, 0), (PART_X, 4), (SUM_Y, 1), (SUM_Y, 2), (NEAR, 0), (A_RING2, 6),
    (PASS_Y, 3), (SUM, 1), (PASS_Y, 4), (FAR_L, 0), (A_RING2, 5), (SUM, 2), (A_RING, 7), (PART_Y, 5),
    (PART_Y, 6), (PASS, 1), (PART_X, 5), (PASS, 2), (PART_X, 6), (D_RING, 2), (SUM, 3), (SUM, 4), (D_RING, 1),
    (A_RING2, 7), (SUM_Y, 3), (PANEL, 1), (SUM_Y, 4), (PAIRS, 0, 0), (PASS_Y, 5), (D_RING2, 1), (PANEL, 2),
    (PAIRS, 0, 1), (PART_Y, 7), (D_RING2, 2), (PART_X, 7), (PASS, 3), (PASS_Y, 6), (PAIRS, 0, 2), (PASS, 4),
    (PAIRS, 0, 3), (SUM_Y, 5), (PANEL, 3), (FAR_R, 1), (SUM, 5), (PANEL, 4), (FAR_R, 2), (SUM_Y, 6),
    (D_RING, 4), (NEAR, 1), (PASS_Y, 7), (NEAR, 2), (D_RING, 3), (D_RING2, 3), (SUM, 6), (D_RING2, 4),
    (PASS, 5), (NEAR, 3), (NEAR, 4), (SUM, 7), (FAR_L, 1), (SUM_Y, 7), (FAR_R, 3), (FAR_L, 2), (D_RING, 6),
    (PANEL, 5), (FAR_R, 4), (D_RING, 5), (PASS, 6), (FAR_L, 3), (D_RING2, 6), (D_RING2, 5), (NEAR, 5),
    (FAR_L, 4), (PASS, 7), (PAIRS, 1, 0), (PAIRS, 1, 1), (PAIRS, 1, 2), (PAIRS, 1, 3), (PANEL, 6),
    (PAIRS, 2, 0), (PAIRS, 2, 1), (PAIRS, 2, 2), (PAIRS, 2, 3), (PANEL, 7), (D_RING, 7), (NEAR, 6),
    (D_RING2, 7), (FAR_R, 5), (PAIRS, 3, 0), (FAR_L, 5), (NEAR, 7), (PAIRS, 3, 1), (PAIRS, 3, 2),
    (PAIRS, 3, 3), (PAIRS, 4, 0), (PAIRS, 4, 1), (PAIRS, 4, 2), (FAR_R, 6), (PAIRS, 4, 3), (FAR_L, 6),
    (FAR_R, 7), (PAIRS, 5, 0), (FAR_L, 7), (PAIRS, 5, 1), (PAIRS, 5, 2), (PAIRS, 5, 3), (PAIRS, 6, 0),
    (PAIRS, 6, 1), (PAIRS, 6, 2), (PAIRS, 6, 3), (PAIRS, 7, 0), (PAIRS, 7, 1), (PAIRS, 7, 2), (PAIRS, 7, 3),
)

MESH = pl.DeviceIdType.MESH
F32 = jnp.float32
BF16 = jnp.bfloat16


def remote(src, dst, send_sem, recv_sem, target):
    return pltpu.make_async_remote_copy(
        src_ref=src, dst_ref=dst, send_sem=send_sem, recv_sem=recv_sem,
        device_id=target, device_id_type=MESH,
    )


def tile_scale(peak):
    return jnp.floor(jnp.log(jnp.maximum(peak, 1e-20) * 1.001) * 1.4426950408889634) + 1.0


def encode(blocks, message):
    peak = None
    for load in blocks:
        for lane in load.lanes:
            high = jnp.abs(load(lane))
            peak = high if peak is None else jnp.maximum(peak, high)
    exponent = tile_scale(peak)
    inverse = jnp.exp2(15.0 - exponent)
    at = 0
    for load in blocks:
        for lane in load.lanes:
            message[at] = (load(lane) * inverse).astype(jnp.int32).astype(jnp.int16)
            at += 1
    message[at] = exponent.astype(jnp.int32).astype(jnp.int16)


def unit(message, last):
    return jnp.exp2(message[last].astype(jnp.int32).astype(F32) - 15.0)


def decode(message, at, scale):
    return message[at].astype(jnp.int32).astype(F32) * scale


class Rows:
    def __init__(self, ref, block, first, lanes):
        self.ref, self.block, self.first, self.lanes = ref, block, first, lanes

    def __call__(self, lane):
        return self.ref[self.block, pl.ds(self.first, HALF), pl.ds(lane, LANE)]


def kernel(
    x3_ref, s3_hbm, prev_hbm, vir_ref, orb_ref, mo_ref, occ_idx, state_idx, slab_rows,
    out_hbm, sig_ref,
    cols, slab, part, x_out, x_in, y_out, y_in, m_out, m_in, n_out, n_in, p_out, p_in, w_out, w_in,
    scr, acc, sg_chip, sg_line, s_ref, wide, relayed, s3_ref, prev_ref, x_ref, few, out_ref,
    a_recv, a_sib, a_send, a_opp, d_recv, d_sib, d_send, d_opp,
    x_send, x_recv, y_send, y_recv, m_send, m_recv, n_send, n_recv, p_send, p_recv, w_send, w_recv,
    c_send, c_recv, g_send, g_recv, l_send, l_recv, r_send, r_recv, load, done,
):
    width = prev_ref.shape[1]
    x_lanes = range(0, width - Y_FIRST * LANE, LANE)
    y_lanes = range(width - Y_FIRST * LANE, width, LANE)
    x_tiles, y_tiles = len(x_lanes), len(y_lanes)
    ri, k = lax.axis_index("ri"), lax.axis_index("occ")
    core = lax.rem(ri, CORE)
    z = lax.rem(ri // CORE, Z)
    hi = ri // (CORE * Z)
    y = lax.rem(k, YS)
    lo = k // YS
    xo = 1 - lo

    def ri_at(h, zz, c):
        return (h * Z + zz) * CORE + c

    def occ_at(x, yy):
        return x * YS + yy

    up = (ri_at(hi, lax.rem(z + 1, Z), core), k)
    down = (ri_at(hi, lax.rem(z + Z - 1, Z), core), k)
    sibling = (ri_at(hi, z, 1 - core), k)
    opposite = (ri_at(1 - hi, z, core), k)
    across = (ri_at(1 - hi, z, 1 - core), k)
    partner = (ri, occ_at(xo, y))
    diagonal = (ri_at(1 - hi, z, core), occ_at(xo, y))
    y_next, y_last, y_far = lax.rem(y + 1, YS), lax.rem(y + YS - 1, YS), lax.rem(y + 2, YS)
    right, left = (ri, occ_at(lo, y_next)), (ri, occ_at(lo, y_last))
    line = [(ri_at(hi, lax.rem(z + s, Z), core), k) for s in range(1, Z)]

    s3_copy = pltpu.make_async_copy(s3_hbm, s3_ref, load.at[0])
    prev_copy = pltpu.make_async_copy(prev_hbm, prev_ref, load.at[1])
    barrier = pltpu.get_barrier_semaphore()
    friends = [sibling, opposite, across, partner, diagonal, right, left] + line
    for friend in friends:
        pl.semaphore_signal(barrier, inc=1, device_id=friend, device_id_type=MESH)

    s3_copy.start()
    prev_copy.start()

    per_sub = prev_ref.shape[0] // (HI * Z * CORE)
    picks = LO * YS * per_sub
    pairs_in, virtual = x3_ref.shape[1:]
    local_rows = [
        lax.rem(slab_rows[kk * prev_ref.shape[0] + ri * per_sub + s], x3_ref.shape[0])
        for kk in range(LO * YS)
        for s in range(per_sub)
    ]
    few_rows = few.reshape(virtual // LANE, picks * 8, LANE)
    for j, row in enumerate(local_rows):
        raw = x3_ref[row].astype(F32)
        for lane in range(0, virtual, LANE):
            few[lane // LANE, j, pl.ds(0, pairs_in), :] = raw[:, lane : lane + LANE]
    for i in range(pairs_in):
        gap = vir_ref[...] - mo_ref[occ_idx[i]]
        weight = 4.0 * gap / (gap * gap + 0.25)
        for lane in range(0, virtual, LANE):
            picked = few_rows[lane // LANE, pl.ds(i, picks, stride=8), :]
            cols[z, core, hi, :, pl.ds(i * virtual + lane, LANE)] = (
                picked * weight[:, lane : lane + LANE]
            ).astype(BF16)

    pl.semaphore_wait(barrier, len(friends))

    a_set = (cols, a_recv, a_sib, a_send, a_opp)
    d_set = (slab, d_recv, d_sib, d_send, d_opp)

    def to_opposite(group):
        buf, recv, sib, send, opp = group
        shard = buf.at[z, core, hi]
        return remote(shard, shard, opp.at[0], recv.at[z, hi], opposite)

    def to_line(group, zz, h, way):
        buf, recv, sib, send, opp = group
        shard = buf.at[zz, core, h]
        return remote(shard, shard, send.at[zz, h, way], recv.at[zz, h], (up, down)[way])

    def to_sibling(group, zz, h):
        buf, recv, sib, send, opp = group
        shard = buf.at[zz, core, h]
        return remote(shard, shard, send.at[zz, h, 2], sib.at[zz, h], sibling)

    def await_shard(group, zz, h):
        buf, recv, sib, send, opp = group
        shard = buf.at[zz, core, h]
        remote(shard, shard, send.at[zz, h, 0], recv.at[zz, h], up).wait_recv()

    def await_sibling(group, zz):
        buf, recv, sib, send, opp = group
        for h in range(HI):
            shard = buf.at[zz, 1 - core, h]
            remote(shard, shard, send.at[zz, h, 2], sib.at[zz, h], sibling).wait_recv()

    def ring(group, c, far, act, arrive):
        zz = chunk_z(c)
        h = 1 - hi if far else hi
        way = (c + 1) % 2
        if arrive:
            await_shard(group, zz, h)
        if c < 5 or (c < 7 and way == far):
            act(to_line(group, zz, h, way))

        act(to_sibling(group, zz, h))

    def start(copy):
        copy.start()

    def finish(copy):
        copy.wait_send()

    def chunk_z(t):
        if isinstance(t, int):
            return lax.rem(z + (Z - (t + 1) // 2 if t % 2 else t // 2), Z)
        return lax.rem(z + jnp.where(lax.rem(t, 2) == 1, Z - (t + 1) // 2, t // 2), Z)

    def products(t, lanes):
        zz = chunk_z(t)
        shards = CORE * HI
        lhs = cols[zz].reshape(shards * picks, cols.shape[-1])
        step = 256
        for first in range(lanes.start, lanes.stop, step):
            res = lax.dot_general(
                lhs, x_ref[pl.ds(first, step), :], (((1,), (1,)), ((), ())),
                preferred_element_type=F32,
            )
            for kk in range(LO * YS):
                for g in range(shards):
                    part[t * (LO * YS) + kk, pl.ds(g * 8, 8), pl.ds(first, step)] = res[
                        g * picks + kk * 8 : g * picks + kk * 8 + 8
                    ]

    def part_y(t):
        await_sibling(a_set, chunk_z(t))
        products(t, y_lanes)
        for way in range(2):
            beside = (y_next, y_last)[way]
            blocks = [Rows(part, at(t, lx, y_far), way * HALF, y_lanes) for lx in range(LO)]
            blocks += [Rows(part, at(t, lx, beside), (1 - way) * HALF, y_lanes) for lx in range(LO)]
            encode(blocks, n_out.at[t, way])
            n_copy(t, way).start()

    def part_x(t):
        products(t, x_lanes)
        blocks = []
        for yy in range(YS):
            for first in (0, HALF):
                blocks.append(Rows(part, at(t, xo, yy), first, x_lanes))
        encode(blocks, x_out.at[t])
        x_copy(t).start()

    def n_copy(t, way):
        return remote(
            n_out.at[t, way], n_in.at[t, way], n_send.at[t, way], n_recv.at[t, way], (right, left)[way]
        )

    def p_copy(t, way):
        return remote(
            p_out.at[t, way], p_in.at[t, way], p_send.at[t, way], p_recv.at[t, way], (right, left)[way]
        )

    def w_copy(t):
        return remote(w_out.at[t], w_in.at[t], w_send.at[t], w_recv.at[t], partner)

    def x_copy(t):
        return remote(x_out.at[t], x_in.at[t], x_send.at[t], x_recv.at[t], partner)

    def y_copy(t, way):
        return remote(
            y_out.at[t, way], y_in.at[t, way], y_send.at[t, way], y_recv.at[t, way], (right, left)[way]
        )

    def m_copy(t, way):
        return remote(
            m_out.at[t, way], m_in.at[t, way], m_send.at[t, way], m_recv.at[t, way], (right, left)[way]
        )

    def c_copy(t, block, lane, target):
        spot = scr.at[t, block]
        return remote(spot, spot, c_send.at[t, lane], c_recv.at[t, block], target)

    def at(t, lx, yy):
        return t * (LO * YS) + occ_at(lx, yy)

    def add(block, first, lanes, message, tile, scale):
        for lane in lanes:
            spot = (block, pl.ds(first, HALF), pl.ds(lane, LANE))
            part[spot] = part[spot] + decode(message, tile, scale)
            tile += 1

    def pair_sum(t):
        x_copy(t).wait_recv()
        message = x_in.at[t]
        scale = unit(message, YS * 2 * x_tiles)
        for yy in range(YS):
            for half in range(2):
                add(at(t, lo, yy), half * HALF, x_lanes, message, (yy * 2 + half) * x_tiles, scale)
        for way in range(2):
            beside = (y_next, y_last)[way]
            encode(
                [
                    Rows(part, at(t, lo, y_far), way * HALF, x_lanes),
                    Rows(part, at(t, lo, beside), (1 - way) * HALF, x_lanes),
                ],
                y_out.at[t, way],
            )
            y_copy(t, way).start()

    def pass_on(t):
        for way in range(2):
            beside = (y_next, y_last)[way]
            y_copy(t, way).wait_recv()
            message = y_in.at[t, way]
            add(at(t, lo, beside), way * HALF, x_lanes, message, 0, unit(message, 2 * x_tiles))
            encode([Rows(part, at(t, lo, beside), way * HALF, x_lanes)], m_out.at[t, way])
            m_copy(t, way).start()

    def pass_on_y(t):
        for way in range(2):
            beside = (y_next, y_last)[way]
            n_copy(t, way).wait_recv()
            message = n_in.at[t, way]
            scale = unit(message, 2 * LO * y_tiles)
            for lx in range(LO):
                add(at(t, lx, beside), way * HALF, y_lanes, message, lx * y_tiles, scale)
            encode(
                [Rows(part, at(t, lx, beside), way * HALF, y_lanes) for lx in range(LO)], p_out.at[t, way]
            )
            p_copy(t, way).start()

    def sum_y(t):
        for way in range(2):
            p_copy(t, way).wait_recv()
        for half in range(2):
            near, far = n_in.at[t, 1 - half], p_in.at[t, half]
            near_scale, far_scale = unit(near, 2 * LO * y_tiles), unit(far, LO * y_tiles)
            for lx in range(LO):
                add(at(t, lx, y), half * HALF, y_lanes, near, (LO + lx) * y_tiles, near_scale)
                add(at(t, lx, y), half * HALF, y_lanes, far, lx * y_tiles, far_scale)
        encode([Rows(part, at(t, xo, y), half * HALF, y_lanes) for half in range(2)], w_out.at[t])
        w_copy(t).start()

    def panel(t):
        zz = chunk_z(t)
        for way in range(2):
            m_copy(t, way).wait_recv()
        w_copy(t).wait_recv()
        if t == 0:
            prev_copy.wait()
        other = w_in.at[t]
        other_scale = unit(other, 2 * y_tiles)
        for half in range(2):
            near, far = y_in.at[t, 1 - half], m_in.at[t, half]
            near_scale, far_scale = unit(near, 2 * x_tiles), unit(far, x_tiles)
            for lane in range(0, width, LANE):
                total = part[at(t, lo, y), pl.ds(half * HALF, HALF), pl.ds(lane, LANE)]
                tile = lane // LANE
                if tile < x_tiles:
                    total = total + decode(near, x_tiles + tile, near_scale)
                    total = total + decode(far, tile, far_scale)
                else:
                    total = total + decode(other, half * y_tiles + tile - x_tiles, other_scale)
                kept = []
                for h in range(HI):
                    row = pl.multiple_of(h * (Z * CORE * 8) + zz * (CORE * 8) + half * 8, 8)
                    value = prev_ref[pl.ds(row, 8), pl.ds(lane, LANE)] - total[h * 8 : h * 8 + 8]
                    out_ref[pl.ds(row, 8), pl.ds(lane, LANE)] = value
                    kept.append(value)
                scr[t, k, pl.ds(half * HALF, HALF), pl.ds(lane, LANE)] = jnp.concatenate(
                    kept, axis=0
                ).astype(BF16)
        for h in range(HI):
            store(t, h).start()
        c_copy(t, k, 0, partner).start()
        c_copy(t, k, 1, right).start()
        c_copy(t, k, 2, left).start()

    def store(t, h):
        deep = CORE * 8
        rows = pl.ds(pl.multiple_of((h * Z + chunk_z(t)) * deep, deep), deep)
        return pltpu.make_async_copy(out_ref.at[rows], out_hbm.at[rows], done.at[t, h])

    def await_block(t, block):
        c_copy(t, block, 0, partner).wait_recv()

    def spread_partner(t):
        block = occ_at(xo, y)
        await_block(t, block)
        c_copy(t, block, 3, right).start()
        c_copy(t, block, 4, left).start()

    def spread_right(t):
        block = occ_at(lo, y_last)
        await_block(t, block)
        c_copy(t, block, 5, right).start()

    def spread_left(t):
        block = occ_at(xo, y_next)
        await_block(t, block)
        c_copy(t, block, 6, left).start()

    def energy(t, quarter):
        zz = chunk_z(t)
        if quarter == 0:
            for block in (occ_at(xo, y_last), occ_at(lo, y_next), occ_at(lo, y_far), occ_at(xo, y_far)):
                await_block(t, block)
            await_sibling(d_set, zz)
        lhs = scr[t].reshape(LO * YS * 2 * HALF, width)
        step = s_ref.shape[1] // 4
        lanes = pl.ds(quarter * step, step)
        applied = jnp.dot(lhs, s_ref[:, lanes], preferred_element_type=F32)
        total = acc[:, lanes]
        for g in range(CORE * HI):
            rows = slab[zz, g // HI, g % HI, :, lanes].astype(F32)
            for kk in range(LO * YS):
                spot = kk * 2 * HALF + g * 8
                total = total + applied[spot : spot + 8] * rows[kk * 8 : kk * 8 + 8]
        acc[:, lanes] = total

    start(to_opposite(a_set))
    start(to_line(a_set, z, hi, 0))
    start(to_line(a_set, z, hi, 1))
    start(to_sibling(a_set, z, hi))

    depth = wide.shape[0] // 8
    wide_rows = wide.reshape(depth, 8, LANE)

    def spread_block(n):
        at_row = n * depth
        for lane in range(0, virtual, LANE):
            wide_rows[:, pl.ds(0, pairs_in), :] = x3_ref[pl.ds(at_row, depth), :, pl.ds(lane, LANE)].astype(F32)
            for i in range(pairs_in):
                x_ref[pl.ds(at_row, depth), pl.ds(i * virtual + lane, LANE)] = wide[
                    pl.ds(i, depth, stride=8), :
                ].astype(BF16)

    acc[...] = jnp.zeros_like(acc)

    def to_diagonal():
        return remote(slab.at[z, core, hi], relayed, r_send.at[0], r_recv.at[0], diagonal)

    def relay_on():
        return remote(relayed, slab.at[z, core, 1 - hi], d_opp.at[0], d_recv.at[z, 1 - hi], partner)

    states, orbitals = s3_ref.shape[1:]
    assert states == 8

    def prepare_states(t):
        s3_copy.wait()
        for j, row in enumerate(local_rows):
            raw = s3_ref[row].astype(F32)
            for lane in range(0, orbitals, LANE):
                few[lane // LANE, j] = raw[:, lane : lane + LANE]
        for state in range(states):
            for lane in range(0, orbitals, LANE):
                slab[z, core, hi, :, pl.ds(state * orbitals + lane, LANE)] = few_rows[
                    lane // LANE, pl.ds(state, picks, stride=8), :
                ].astype(BF16)
        start(to_diagonal())

    def spread_states(n):
        at_row = n * depth
        for lane in range(0, orbitals, LANE):
            raw = s3_ref[pl.ds(at_row, depth), :, pl.ds(lane, LANE)].astype(F32)
            wide[...] = raw.reshape(depth * states, LANE)
            for state in range(states):
                s_ref[pl.ds(at_row, depth), pl.ds(state * orbitals + lane, LANE)] = wide[
                    pl.ds(state, depth, stride=states), :
                ].astype(BF16)

    def relay(t):
        to_diagonal().wait_recv()
        start(relay_on())

    def first_far(group):
        await_shard(group, z, 1 - hi)
        start(to_sibling(group, z, 1 - hi))
        start(to_line(group, z, 1 - hi, 0))
        start(to_line(group, z, 1 - hi, 1))

    def first_own(t):
        start(to_sibling(d_set, z, hi))
        start(to_line(d_set, z, hi, 0))
        start(to_line(d_set, z, hi, 1))

    stages = {
        RELAY: relay,
        A_OPP: lambda t: first_far(a_set),
        D_OWN: first_own,
        D_OPP: lambda t: first_far(d_set),
        A_RING: lambda t: ring(a_set, t, 0, start, True),
        A_RING2: lambda t: ring(a_set, t, 1, start, True),
        D_RING: lambda t: ring(d_set, t, 0, start, True),
        D_RING2: lambda t: ring(d_set, t, 1, start, True),
        D_PREP: prepare_states,
        X_SPREAD: spread_block,
        S_SPREAD: spread_states,
        PART_Y: part_y,
        PART_X: part_x,
        SUM: pair_sum,
        PASS: pass_on,
        PASS_Y: pass_on_y,
        SUM_Y: sum_y,
        PANEL: panel,
        NEAR: spread_partner,
        FAR_R: spread_right,
        FAR_L: spread_left,
        PAIRS: energy,
    }

    for stage, *spot in ORDER:
        stages[stage](*spot)

    pairs = jnp.sum(acc[...], axis=0, keepdims=True)
    mine = hi * CORE + core
    for n in range(state_idx.shape[0]):
        gap = mo_ref[state_idx[n]] - orb_ref[...]
        factor = gap / (gap * gap + 0.25)
        value = jnp.sum(factor * pairs[:, n * orbitals : (n + 1) * orbitals], axis=1, keepdims=True)
        sg_chip[mine, pl.ds(n, 1), :] = jnp.broadcast_to(value, (1, LANE))

    def chip_copy(n, target):
        spot = sg_chip.at[mine]
        return remote(spot, spot, g_send.at[n], g_recv.at[mine], target)

    chip = [
        (sibling, hi * CORE + 1 - core),
        (opposite, (1 - hi) * CORE + core),
        (across, (1 - hi) * CORE + 1 - core),
    ]
    for n, (target, slot) in enumerate(chip):
        chip_copy(n, target).start()
    finish(to_opposite(a_set))
    finish(to_diagonal())
    finish(relay_on())
    for group in (a_set, d_set):
        for h in range(HI):
            finish(to_line(group, z, h, 0))
            finish(to_line(group, z, h, 1))
            finish(to_sibling(group, z, h))

        for c in range(1, CHUNKS):
            ring(group, c, 0, finish, False)
            ring(group, c, 1, finish, False)

    def drain(t, carry):
        x_copy(t).wait_send()
        for way in range(2):
            y_copy(t, way).wait_send()
            m_copy(t, way).wait_send()
            n_copy(t, way).wait_send()
            p_copy(t, way).wait_send()
        w_copy(t).wait_send()
        for h in range(HI):
            store(t, h).wait()
        for lane in range(7):
            c_copy(t, k, lane, partner).wait_send()
        return carry

    lax.fori_loop(0, CHUNKS // 2, drain, 0)
    for n, (target, slot) in enumerate(chip):
        spot = sg_chip.at[slot]
        remote(spot, spot, g_send.at[n], g_recv.at[slot], target).wait_recv()
    sg_line[z] = (sg_chip[0] + sg_chip[1]) + (sg_chip[2] + sg_chip[3])

    def line_copy(n, target):
        spot = sg_line.at[z]
        return remote(spot, spot, l_send.at[n], l_recv.at[z], target)

    for n, target in enumerate(line):
        line_copy(n, target).start()
    lax.fori_loop(CHUNKS // 2, CHUNKS, drain, 0)
    for n, target in enumerate(line):
        slot = lax.rem(z + 1 + n, Z)
        spot = sg_line.at[slot]
        remote(spot, spot, l_send.at[n], l_recv.at[slot], target).wait_recv()
    total = sg_line[0]
    for n in range(1, Z):
        total = total + sg_line[n]
    diag = lax.broadcasted_iota(jnp.int32, total.shape, 0) == lax.broadcasted_iota(jnp.int32, total.shape, 1)
    sig_ref[...] = jnp.sum(jnp.where(diag, total, 0.0), axis=0, keepdims=True)[:, : sig_ref.shape[1]]

    for n, (target, slot) in enumerate(chip):
        chip_copy(n, target).wait_send()
    for n, target in enumerate(line):
        line_copy(n, target).wait_send()


def hand_over(panel_in, sig_in, panel_out, sig_out):
    panel_out[...] = panel_in[...]
    sig_out[...] = sig_in[...]


def local(
    three_index,
    polar_prev,
    states,
    mo_energy,
    vir_energy,
    orbital_energy,
    occ_index,
    state_index,
    slab_rows,
):
    ri_count = lax.axis_size("ri")
    occ_count = lax.axis_size("occ")
    assert (ri_count, occ_count) == (HI * Z * CORE, LO * YS)
    p_dev = three_index.shape[0]
    col_block = polar_prev.shape[0]
    picks = slab_rows.shape[0] // ri_count
    ns_dev, orbitals = states.shape[1:]
    pairs = three_index.shape[1] * three_index.shape[2]
    spread = ns_dev * orbitals
    y_tiles = Y_FIRST
    x_tiles = p_dev // LANE - Y_FIRST

    def message(count, *lead):
        return pltpu.VMEM((CHUNKS, *lead, count + 1, HALF, LANE), jnp.int16)

    vmem = pl.BlockSpec(memory_space=pltpu.VMEM)
    hbm = pl.BlockSpec(memory_space=pl.ANY)
    smem = pl.BlockSpec(memory_space=pltpu.SMEM)
    dma = pltpu.SemaphoreType.DMA
    ring_sems = [dma((Z, HI)), dma((Z, HI)), dma((Z, HI, 3)), dma((1,))]
    panel_out, sig = pl.pallas_call(
        kernel,
        out_shape=(
            jax.ShapeDtypeStruct((col_block, p_dev), F32),
            jax.ShapeDtypeStruct((1, ns_dev), F32),
        ),
        in_specs=[vmem, hbm, hbm, vmem, vmem] + [smem] * 4,
        out_specs=(hbm, vmem),
        scratch_shapes=[
            pltpu.VMEM((Z, CORE, HI, picks, pairs), BF16),
            pltpu.VMEM((Z, CORE, HI, picks, spread), BF16),
            pltpu.VMEM((CHUNKS * occ_count, 2 * HALF, p_dev), F32),
            message(YS * 2 * x_tiles), message(YS * 2 * x_tiles),
            message(2 * x_tiles, 2), message(2 * x_tiles, 2),
            message(x_tiles, 2), message(x_tiles, 2),
            message(2 * LO * y_tiles, 2), message(2 * LO * y_tiles, 2),
            message(LO * y_tiles, 2), message(LO * y_tiles, 2),
            message(2 * y_tiles), message(2 * y_tiles),
            pltpu.VMEM((CHUNKS, occ_count, 2 * HALF, p_dev), BF16),
            pltpu.VMEM((8, spread), F32),
            pltpu.VMEM((HI * CORE, 8, LANE), F32),
            pltpu.VMEM((Z, 8, LANE), F32),
            pltpu.VMEM((p_dev, spread), BF16),
            pltpu.VMEM((LANE * ns_dev, LANE), F32),
            pltpu.VMEM((picks, spread), BF16),
            pltpu.VMEM((p_dev, ns_dev, orbitals), BF16),
            pltpu.VMEM((col_block, p_dev), F32),
            pltpu.VMEM((p_dev, pairs), BF16),
            pltpu.VMEM((three_index.shape[2] // LANE, picks, 8, LANE), F32),
            pltpu.VMEM((col_block, p_dev), F32),
            *ring_sems,
            *ring_sems,
            dma((CHUNKS,)), dma((CHUNKS,)),
            dma((CHUNKS, 2)), dma((CHUNKS, 2)),
            dma((CHUNKS, 2)), dma((CHUNKS, 2)),
            dma((CHUNKS, 2)), dma((CHUNKS, 2)),
            dma((CHUNKS, 2)), dma((CHUNKS, 2)),
            dma((CHUNKS,)), dma((CHUNKS,)),
            dma((CHUNKS, 7)), dma((CHUNKS, occ_count)),
            dma((3,)), dma((HI * CORE,)),
            dma((Z - 1,)), dma((Z,)),
            dma((1,)), dma((1,)), dma((2,)), dma((CHUNKS, HI)),
        ],
        compiler_params=pltpu.CompilerParams(
            collective_id=0, has_side_effects=True, vmem_limit_bytes=60 * 2**20
        ),
        cost_estimate=pl.CostEstimate(
            flops=13 * 10**9, bytes_accessed=9 * 2**20, transcendentals=0
        ),
    )(
        three_index, states, polar_prev,
        vir_energy.reshape(1, -1), orbital_energy.reshape(1, -1),
        mo_energy, occ_index, state_index, slab_rows,
    )
    panel_out, sig = pl.pallas_call(
        hand_over,
        out_shape=(
            jax.ShapeDtypeStruct((col_block, p_dev), F32),
            jax.ShapeDtypeStruct((1, ns_dev), F32),
        ),
        in_specs=[vmem, vmem],
        out_specs=(vmem, vmem),
    )(panel_out, sig)
    return (panel_out, sig.reshape(ns_dev))


def solution(mesh):
    in_specs = (
        P("ri", "occ", None),
        P("occ", "ri"),
        P("ri", "occ", None),
        P(),
        P(),
        P(),
        P("occ"),
        P("occ"),
        P(),
    )
    out_specs = (P("occ", "ri"), P("occ"))
    return jax.shard_map(local, mesh=mesh, in_specs=in_specs, out_specs=out_specs, check_vma=False)
```

```python
import jax
import jax.numpy as jnp
from jax import lax
from jax.experimental import pallas as pl
from jax.experimental.pallas import tpu as pltpu
from jax.sharding import PartitionSpec as P

HI, Z, CORE, LO, YS = 2, 8, 2, 2, 4
CHUNKS = Z
LANE = 128
HALF = 16
VIA_X = (0, 1, 2, 3)
Y_FIRST = 4

(
    RELAY, A_OPP, D_PREP, D_OWN, D_OPP, A_RING, A_RING2, D_RING, D_RING2, PART_Y, PART_X, SUM, PASS, PASS_Y,
    SUM_Y, PANEL, NEAR, FAR_R, FAR_L, PAIRS, X_SPREAD, S_SPREAD,
) = range(22)
ORDER = (
    (D_PREP, 0), (X_SPREAD, 4), (X_SPREAD, 5), (X_SPREAD, 6), (X_SPREAD, 7), (X_SPREAD, 0), (X_SPREAD, 1),
    (A_RING, 1), (A_RING, 2), (X_SPREAD, 2), (X_SPREAD, 3), (A_OPP, 0), (S_SPREAD, 0), (S_SPREAD, 1),
    (RELAY, 0), (PART_Y, 0), (PART_X, 0), (S_SPREAD, 2), (A_RING, 3), (A_RING, 4), (S_SPREAD, 3),
    (A_RING2, 1), (A_RING2, 2), (PASS_Y, 0), (S_SPREAD, 4), (S_SPREAD, 5), (PART_Y, 1), (PART_Y, 2),
    (PART_X, 1), (PART_X, 2), (SUM, 0), (A_RING, 5), (A_RING2, 3), (A_RING2, 4), (A_RING, 6), (SUM_Y, 0),
    (S_SPREAD, 6), (PASS_Y, 1), (S_SPREAD, 7), (PASS, 0), (PASS_Y, 2), (PART_Y, 3), (PART_Y, 4), (D_OWN, 0),
    (PART_X, 3), (PANEL, 0), (PART_X, 4), (SUM, 1), (A_RING2, 6), (SUM, 2), (A_RING2, 5), (A_RING, 7),
    (SUM_Y, 1), (SUM_Y, 2), (D_OPP, 0), (PASS_Y, 3), (PART_Y, 5), (PART_Y, 6), (PART_X, 5), (PASS, 1),
    (NEAR, 0), (PASS, 2), (PART_X, 6), (SUM_Y, 3), (PASS_Y, 4), (D_RING, 1), (PANEL, 1), (A_RING2, 7),
    (PANEL, 2), (SUM, 3), (PASS_Y, 5), (D_RING, 2), (PASS_Y, 6), (PART_Y, 7), (PART_X, 7), (D_RING2, 1),
    (SUM, 4), (SUM_Y, 4), (FAR_L, 0), (D_RING2, 2), (PASS, 3), (SUM_Y, 5), (SUM_Y, 6), (NEAR, 1), (FAR_R, 1),
    (NEAR, 2), (D_RING, 3), (PASS, 4), (SUM, 5), (PANEL, 3), (PASS_Y, 7), (D_RING, 4), (SUM, 6), (FAR_R, 0),
    (PANEL, 4), (D_RING2, 3), (SUM, 7), (D_RING2, 4), (NEAR, 3), (FAR_L, 1), (PASS, 5), (FAR_L, 2),
    (PAIRS, 0, 0), (PAIRS, 0, 1), (NEAR, 4), (PAIRS, 0, 2), (SUM_Y, 7), (PAIRS, 0, 3), (PASS, 6),
    (PAIRS, 1, 0), (PAIRS, 1, 1), (PAIRS, 1, 2), (PAIRS, 1, 3), (FAR_R, 3), (D_RING, 5), (PANEL, 5),
    (PASS, 7), (FAR_R, 4), (D_RING, 6), (PANEL, 6), (NEAR, 5), (D_RING2, 5), (D_RING2, 6), (PANEL, 7),
    (NEAR, 6), (FAR_R, 2), (FAR_L, 4), (D_RING, 7), (NEAR, 7), (FAR_L, 3), (PAIRS, 2, 0), (PAIRS, 2, 1),
    (PAIRS, 2, 2), (FAR_R, 5), (PAIRS, 2, 3), (D_RING2, 7), (PAIRS, 3, 0), (FAR_L, 5), (PAIRS, 3, 1),
    (FAR_R, 6), (PAIRS, 3, 2), (PAIRS, 3, 3), (FAR_L, 6), (PAIRS, 4, 0), (PAIRS, 4, 1), (FAR_R, 7),
    (PAIRS, 4, 2), (FAR_L, 7), (PAIRS, 4, 3), (PAIRS, 5, 0), (PAIRS, 5, 1), (PAIRS, 5, 2), (PAIRS, 5, 3),
    (PAIRS, 6, 0), (PAIRS, 6, 1), (PAIRS, 6, 2), (PAIRS, 6, 3), (PAIRS, 7, 0), (PAIRS, 7, 1), (PAIRS, 7, 2),
    (PAIRS, 7, 3),
)

MESH = pl.DeviceIdType.MESH
F32 = jnp.float32
BF16 = jnp.bfloat16


def remote(src, dst, send_sem, recv_sem, target):
    return pltpu.make_async_remote_copy(
        src_ref=src, dst_ref=dst, send_sem=send_sem, recv_sem=recv_sem,
        device_id=target, device_id_type=MESH,
    )


def tile_scale(peak):
    return jnp.floor(jnp.log(jnp.maximum(peak, 1e-20) * 1.001) * 1.4426950408889634) + 1.0


def encode(blocks, message):
    peak = None
    for load in blocks:
        for lane in load.lanes:
            high = jnp.abs(load(lane))
            peak = high if peak is None else jnp.maximum(peak, high)
    exponent = tile_scale(peak)
    inverse = jnp.exp2(15.0 - exponent)
    at = 0
    for load in blocks:
        for lane in load.lanes:
            message[at] = (load(lane) * inverse).astype(jnp.int32).astype(jnp.int16)
            at += 1
    message[at] = exponent.astype(jnp.int32).astype(jnp.int16)


def unit(message, last):
    return jnp.exp2(message[last].astype(jnp.int32).astype(F32) - 15.0)


def decode(message, at, scale):
    return message[at].astype(jnp.int32).astype(F32) * scale


class Rows:
    def __init__(self, ref, block, first, lanes):
        self.ref, self.block, self.first, self.lanes = ref, block, first, lanes

    def __call__(self, lane):
        return self.ref[self.block, pl.ds(self.first, HALF), pl.ds(lane, LANE)]


def kernel(
    x3_hbm, s3_hbm, prev_hbm, vir_ref, orb_ref, mo_ref, occ_idx, state_idx, slab_rows,
    out_hbm, sig_ref,
    cols, slab, part, x_out, x_in, y_out, y_in, m_out, m_in, n_out, n_in, p_out, p_in, w_out, w_in,
    scr, acc, sg_chip, sg_line, s_ref, wide, relayed, s3_ref, prev_ref, x_ref, few, out_ref, x3_ref,
    a_recv, a_sib, a_send, a_opp, d_recv, d_sib, d_send, d_opp,
    x_send, x_recv, y_send, y_recv, m_send, m_recv, n_send, n_recv, p_send, p_recv, w_send, w_recv,
    c_send, c_recv, g_send, g_recv, l_send, l_recv, r_send, r_recv, load, done,
):
    width = prev_ref.shape[1]
    x_lanes = range(0, width - Y_FIRST * LANE, LANE)
    y_lanes = range(width - Y_FIRST * LANE, width, LANE)
    x_tiles, y_tiles = len(x_lanes), len(y_lanes)
    ri, k = lax.axis_index("ri"), lax.axis_index("occ")
    core = lax.rem(ri, CORE)
    z = lax.rem(ri // CORE, Z)
    hi = ri // (CORE * Z)
    y = lax.rem(k, YS)
    lo = k // YS
    xo = 1 - lo

    def ri_at(h, zz, c):
        return (h * Z + zz) * CORE + c

    def occ_at(x, yy):
        return x * YS + yy

    up = (ri_at(hi, lax.rem(z + 1, Z), core), k)
    down = (ri_at(hi, lax.rem(z + Z - 1, Z), core), k)
    sibling = (ri_at(hi, z, 1 - core), k)
    opposite = (ri_at(1 - hi, z, core), k)
    across = (ri_at(1 - hi, z, 1 - core), k)
    partner = (ri, occ_at(xo, y))
    diagonal = (ri_at(1 - hi, z, core), occ_at(xo, y))
    y_next, y_last, y_far = lax.rem(y + 1, YS), lax.rem(y + YS - 1, YS), lax.rem(y + 2, YS)
    right, left = (ri, occ_at(lo, y_next)), (ri, occ_at(lo, y_last))
    line = [(ri_at(hi, lax.rem(z + s, Z), core), k) for s in range(1, Z)]

    s3_copy = pltpu.make_async_copy(s3_hbm, s3_ref, load.at[0])
    prev_copy = pltpu.make_async_copy(prev_hbm, prev_ref, load.at[1])
    x3_copy = pltpu.make_async_copy(x3_hbm, x3_ref, load.at[2])
    x3_copy.start()
    barrier = pltpu.get_barrier_semaphore()
    friends = [sibling, opposite, across, partner, diagonal, right, left] + line
    for friend in friends:
        pl.semaphore_signal(barrier, inc=1, device_id=friend, device_id_type=MESH)

    x3_copy.wait()
    s3_copy.start()
    prev_copy.start()

    per_sub = prev_ref.shape[0] // (HI * Z * CORE)
    picks = LO * YS * per_sub
    pairs_in, virtual = x3_ref.shape[1:]
    local_rows = [
        lax.rem(slab_rows[kk * prev_ref.shape[0] + ri * per_sub + s], x3_ref.shape[0])
        for kk in range(LO * YS)
        for s in range(per_sub)
    ]
    few_rows = few.reshape(virtual // LANE, picks * 8, LANE)
    for j, row in enumerate(local_rows):
        raw = x3_ref[row].astype(F32)
        for lane in range(0, virtual, LANE):
            few[lane // LANE, j, pl.ds(0, pairs_in), :] = raw[:, lane : lane + LANE]
    for i in range(pairs_in):
        gap = vir_ref[...] - mo_ref[occ_idx[i]]
        weight = 4.0 * gap / (gap * gap + 0.25)
        for lane in range(0, virtual, LANE):
            picked = few_rows[lane // LANE, pl.ds(i, picks, stride=8), :]
            cols[z, core, hi, :, pl.ds(i * virtual + lane, LANE)] = (
                picked * weight[:, lane : lane + LANE]
            ).astype(BF16)

    pl.semaphore_wait(barrier, len(friends))

    a_set = (cols, a_recv, a_sib, a_send, a_opp)
    d_set = (slab, d_recv, d_sib, d_send, d_opp)

    def to_opposite(group):
        buf, recv, sib, send, opp = group
        shard = buf.at[z, core, hi]
        return remote(shard, shard, opp.at[0], recv.at[z, hi], opposite)

    def to_line(group, zz, h, way):
        buf, recv, sib, send, opp = group
        shard = buf.at[zz, core, h]
        return remote(shard, shard, send.at[zz, h, way], recv.at[zz, h], (up, down)[way])

    def to_sibling(group, zz, h):
        buf, recv, sib, send, opp = group
        shard = buf.at[zz, core, h]
        return remote(shard, shard, send.at[zz, h, 2], sib.at[zz, h], sibling)

    def await_shard(group, zz, h):
        buf, recv, sib, send, opp = group
        shard = buf.at[zz, core, h]
        remote(shard, shard, send.at[zz, h, 0], recv.at[zz, h], up).wait_recv()

    def await_sibling(group, zz):
        buf, recv, sib, send, opp = group
        for h in range(HI):
            shard = buf.at[zz, 1 - core, h]
            remote(shard, shard, send.at[zz, h, 2], sib.at[zz, h], sibling).wait_recv()

    def ring(group, c, far, act, arrive):
        zz = chunk_z(c)
        h = 1 - hi if far else hi
        way = (c + 1) % 2
        if arrive:
            await_shard(group, zz, h)
        if c < 5 or (c < 7 and way == far):
            act(to_line(group, zz, h, way))

        act(to_sibling(group, zz, h))

    def start(copy):
        copy.start()

    def finish(copy):
        copy.wait_send()

    def chunk_z(t):
        if isinstance(t, int):
            return lax.rem(z + (Z - (t + 1) // 2 if t % 2 else t // 2), Z)
        return lax.rem(z + jnp.where(lax.rem(t, 2) == 1, Z - (t + 1) // 2, t // 2), Z)

    def products(t, lanes):
        zz = chunk_z(t)
        shards = CORE * HI
        lhs = cols[zz].reshape(shards * picks, cols.shape[-1])
        step = 256
        for first in range(lanes.start, lanes.stop, step):
            res = lax.dot_general(
                lhs, x_ref[pl.ds(first, step), :], (((1,), (1,)), ((), ())),
                preferred_element_type=F32,
            )
            for kk in range(LO * YS):
                for g in range(shards):
                    part[t * (LO * YS) + kk, pl.ds(g * 8, 8), pl.ds(first, step)] = res[
                        g * picks + kk * 8 : g * picks + kk * 8 + 8
                    ]

    def part_y(t):
        await_sibling(a_set, chunk_z(t))
        products(t, y_lanes)
        for way in range(2):
            beside = (y_next, y_last)[way]
            blocks = [Rows(part, at(t, lx, y_far), way * HALF, y_lanes) for lx in range(LO)]
            blocks += [Rows(part, at(t, lx, beside), (1 - way) * HALF, y_lanes) for lx in range(LO)]
            encode(blocks, n_out.at[t, way])
            n_copy(t, way).start()

    def part_x(t):
        products(t, x_lanes)
        blocks = []
        for yy in range(YS):
            for first in (0, HALF):
                blocks.append(Rows(part, at(t, xo, yy), first, x_lanes))
        encode(blocks, x_out.at[t])
        x_copy(t).start()

    def n_copy(t, way):
        return remote(
            n_out.at[t, way], n_in.at[t, way], n_send.at[t, way], n_recv.at[t, way], (right, left)[way]
        )

    def p_copy(t, way):
        return remote(
            p_out.at[t, way], p_in.at[t, way], p_send.at[t, way], p_recv.at[t, way], (right, left)[way]
        )

    def w_copy(t):
        return remote(w_out.at[t], w_in.at[t], w_send.at[t], w_recv.at[t], partner)

    def x_copy(t):
        return remote(x_out.at[t], x_in.at[t], x_send.at[t], x_recv.at[t], partner)

    def y_copy(t, way):
        return remote(
            y_out.at[t, way], y_in.at[t, way], y_send.at[t, way], y_recv.at[t, way], (right, left)[way]
        )

    def m_copy(t, way):
        return remote(
            m_out.at[t, way], m_in.at[t, way], m_send.at[t, way], m_recv.at[t, way], (right, left)[way]
        )

    def c_copy(t, block, lane, target):
        spot = scr.at[t, block]
        return remote(spot, spot, c_send.at[t, lane], c_recv.at[t, block], target)

    def at(t, lx, yy):
        return t * (LO * YS) + occ_at(lx, yy)

    def add(block, first, lanes, message, tile, scale):
        for lane in lanes:
            spot = (block, pl.ds(first, HALF), pl.ds(lane, LANE))
            part[spot] = part[spot] + decode(message, tile, scale)
            tile += 1

    def pair_sum(t):
        x_copy(t).wait_recv()
        message = x_in.at[t]
        scale = unit(message, YS * 2 * x_tiles)
        for yy in range(YS):
            for half in range(2):
                add(at(t, lo, yy), half * HALF, x_lanes, message, (yy * 2 + half) * x_tiles, scale)
        for way in range(2):
            beside = (y_next, y_last)[way]
            encode(
                [
                    Rows(part, at(t, lo, y_far), way * HALF, x_lanes),
                    Rows(part, at(t, lo, beside), (1 - way) * HALF, x_lanes),
                ],
                y_out.at[t, way],
            )
            y_copy(t, way).start()

    def pass_on(t):
        for way in range(2):
            beside = (y_next, y_last)[way]
            y_copy(t, way).wait_recv()
            message = y_in.at[t, way]
            add(at(t, lo, beside), way * HALF, x_lanes, message, 0, unit(message, 2 * x_tiles))
            encode([Rows(part, at(t, lo, beside), way * HALF, x_lanes)], m_out.at[t, way])
            m_copy(t, way).start()

    def pass_on_y(t):
        for way in range(2):
            beside = (y_next, y_last)[way]
            n_copy(t, way).wait_recv()
            message = n_in.at[t, way]
            scale = unit(message, 2 * LO * y_tiles)
            for lx in range(LO):
                add(at(t, lx, beside), way * HALF, y_lanes, message, lx * y_tiles, scale)
            encode(
                [Rows(part, at(t, lx, beside), way * HALF, y_lanes) for lx in range(LO)], p_out.at[t, way]
            )
            p_copy(t, way).start()

    def sum_y(t):
        for way in range(2):
            p_copy(t, way).wait_recv()
        for half in range(2):
            near, far = n_in.at[t, 1 - half], p_in.at[t, half]
            near_scale, far_scale = unit(near, 2 * LO * y_tiles), unit(far, LO * y_tiles)
            for lx in range(LO):
                add(at(t, lx, y), half * HALF, y_lanes, near, (LO + lx) * y_tiles, near_scale)
                add(at(t, lx, y), half * HALF, y_lanes, far, lx * y_tiles, far_scale)
        encode([Rows(part, at(t, xo, y), half * HALF, y_lanes) for half in range(2)], w_out.at[t])
        w_copy(t).start()

    def panel(t):
        zz = chunk_z(t)
        for way in range(2):
            m_copy(t, way).wait_recv()
        w_copy(t).wait_recv()
        if t == 0:
            prev_copy.wait()
        other = w_in.at[t]
        other_scale = unit(other, 2 * y_tiles)
        for half in range(2):
            near, far = y_in.at[t, 1 - half], m_in.at[t, half]
            near_scale, far_scale = unit(near, 2 * x_tiles), unit(far, x_tiles)
            for lane in range(0, width, LANE):
                total = part[at(t, lo, y), pl.ds(half * HALF, HALF), pl.ds(lane, LANE)]
                tile = lane // LANE
                if tile < x_tiles:
                    total = total + decode(near, x_tiles + tile, near_scale)
                    total = total + decode(far, tile, far_scale)
                else:
                    total = total + decode(other, half * y_tiles + tile - x_tiles, other_scale)
                kept = []
                for h in range(HI):
                    row = pl.multiple_of(h * (Z * CORE * 8) + zz * (CORE * 8) + half * 8, 8)
                    value = prev_ref[pl.ds(row, 8), pl.ds(lane, LANE)] - total[h * 8 : h * 8 + 8]
                    out_ref[pl.ds(row, 8), pl.ds(lane, LANE)] = value
                    kept.append(value)
                scr[t, k, pl.ds(half * HALF, HALF), pl.ds(lane, LANE)] = jnp.concatenate(
                    kept, axis=0
                ).astype(BF16)
        for h in range(HI):
            store(t, h).start()
        c_copy(t, k, 0, partner).start()
        c_copy(t, k, 1, right).start()
        c_copy(t, k, 2, left).start()

    def store(t, h):
        deep = CORE * 8
        rows = pl.ds(pl.multiple_of((h * Z + chunk_z(t)) * deep, deep), deep)
        return pltpu.make_async_copy(out_ref.at[rows], out_hbm.at[rows], done.at[t, h])

    def await_block(t, block):
        c_copy(t, block, 0, partner).wait_recv()

    def spread_partner(t):
        block = occ_at(xo, y)
        await_block(t, block)
        c_copy(t, block, 3, right).start()
        c_copy(t, block, 4, left).start()

    def spread_right(t):
        if t in VIA_X and t % 2 == 0:
            block, target = occ_at(xo, y_far), partner
        else:
            block, target = occ_at(lo, y_last), right
        await_block(t, block)
        c_copy(t, block, 5, target).start()

    def spread_left(t):
        if t in VIA_X and t % 2 == 1:
            block, target = occ_at(lo, y_far), partner
        else:
            block, target = occ_at(xo, y_next), left
        await_block(t, block)
        c_copy(t, block, 6, target).start()

    def rest(t):
        blocks = [occ_at(xo, y_last), occ_at(lo, y_next)]
        if t in VIA_X and t % 2 == 0:
            blocks += [occ_at(lo, y_last), occ_at(lo, y_far)]
        elif t in VIA_X:
            blocks += [occ_at(xo, y_next), occ_at(xo, y_far)]
        else:
            blocks += [occ_at(lo, y_far), occ_at(xo, y_far)]
        return blocks

    def energy(t, quarter):
        zz = chunk_z(t)
        if quarter == 0:
            for block in rest(t):
                await_block(t, block)
            await_sibling(d_set, zz)
        lhs = scr[t].reshape(LO * YS * 2 * HALF, width)
        step = s_ref.shape[1] // 4
        lanes = pl.ds(quarter * step, step)
        applied = jnp.dot(lhs, s_ref[:, lanes], preferred_element_type=F32)
        total = acc[:, lanes]
        for g in range(CORE * HI):
            rows = slab[zz, g // HI, g % HI, :, lanes].astype(F32)
            for kk in range(LO * YS):
                spot = kk * 2 * HALF + g * 8
                total = total + applied[spot : spot + 8] * rows[kk * 8 : kk * 8 + 8]
        acc[:, lanes] = total

    start(to_opposite(a_set))
    start(to_line(a_set, z, hi, 0))
    start(to_line(a_set, z, hi, 1))
    start(to_sibling(a_set, z, hi))

    depth = wide.shape[0] // 8
    wide_rows = wide.reshape(depth, 8, LANE)

    def spread_block(n):
        at_row = n * depth
        for lane in range(0, virtual, LANE):
            wide_rows[:, pl.ds(0, pairs_in), :] = x3_ref[pl.ds(at_row, depth), :, pl.ds(lane, LANE)].astype(F32)
            for i in range(pairs_in):
                x_ref[pl.ds(at_row, depth), pl.ds(i * virtual + lane, LANE)] = wide[
                    pl.ds(i, depth, stride=8), :
                ].astype(BF16)

    acc[...] = jnp.zeros_like(acc)

    def to_diagonal():
        return remote(slab.at[z, core, hi], relayed, r_send.at[0], r_recv.at[0], diagonal)

    def relay_on():
        return remote(relayed, slab.at[z, core, 1 - hi], d_opp.at[0], d_recv.at[z, 1 - hi], partner)

    states, orbitals = s3_ref.shape[1:]
    assert states == 8

    def prepare_states(t):
        s3_copy.wait()
        for j, row in enumerate(local_rows):
            raw = s3_ref[row].astype(F32)
            for lane in range(0, orbitals, LANE):
                few[lane // LANE, j] = raw[:, lane : lane + LANE]
        for state in range(states):
            for lane in range(0, orbitals, LANE):
                slab[z, core, hi, :, pl.ds(state * orbitals + lane, LANE)] = few_rows[
                    lane // LANE, pl.ds(state, picks, stride=8), :
                ].astype(BF16)
        start(to_diagonal())

    def spread_states(n):
        at_row = n * depth
        for lane in range(0, orbitals, LANE):
            raw = s3_ref[pl.ds(at_row, depth), :, pl.ds(lane, LANE)].astype(F32)
            wide[...] = raw.reshape(depth * states, LANE)
            for state in range(states):
                s_ref[pl.ds(at_row, depth), pl.ds(state * orbitals + lane, LANE)] = wide[
                    pl.ds(state, depth, stride=states), :
                ].astype(BF16)

    def relay(t):
        to_diagonal().wait_recv()
        start(relay_on())

    def first_far(group):
        await_shard(group, z, 1 - hi)
        start(to_sibling(group, z, 1 - hi))
        start(to_line(group, z, 1 - hi, 0))
        start(to_line(group, z, 1 - hi, 1))

    def first_own(t):
        start(to_sibling(d_set, z, hi))
        start(to_line(d_set, z, hi, 0))
        start(to_line(d_set, z, hi, 1))

    stages = {
        RELAY: relay,
        A_OPP: lambda t: first_far(a_set),
        D_OWN: first_own,
        D_OPP: lambda t: first_far(d_set),
        A_RING: lambda t: ring(a_set, t, 0, start, True),
        A_RING2: lambda t: ring(a_set, t, 1, start, True),
        D_RING: lambda t: ring(d_set, t, 0, start, True),
        D_RING2: lambda t: ring(d_set, t, 1, start, True),
        D_PREP: prepare_states,
        X_SPREAD: spread_block,
        S_SPREAD: spread_states,
        PART_Y: part_y,
        PART_X: part_x,
        SUM: pair_sum,
        PASS: pass_on,
        PASS_Y: pass_on_y,
        SUM_Y: sum_y,
        PANEL: panel,
        NEAR: spread_partner,
        FAR_R: spread_right,
        FAR_L: spread_left,
        PAIRS: energy,
    }

    for stage, *spot in ORDER:
        stages[stage](*spot)

    pairs = jnp.sum(acc[...], axis=0, keepdims=True)
    mine = hi * CORE + core
    for n in range(state_idx.shape[0]):
        gap = mo_ref[state_idx[n]] - orb_ref[...]
        factor = gap / (gap * gap + 0.25)
        value = jnp.sum(factor * pairs[:, n * orbitals : (n + 1) * orbitals], axis=1, keepdims=True)
        sg_chip[mine, pl.ds(n, 1), :] = jnp.broadcast_to(value, (1, LANE))

    def chip_copy(n, target):
        spot = sg_chip.at[mine]
        return remote(spot, spot, g_send.at[n], g_recv.at[mine], target)

    chip = [
        (sibling, hi * CORE + 1 - core),
        (opposite, (1 - hi) * CORE + core),
        (across, (1 - hi) * CORE + 1 - core),
    ]
    for n, (target, slot) in enumerate(chip):
        chip_copy(n, target).start()
    finish(to_opposite(a_set))
    finish(to_diagonal())
    finish(relay_on())
    for group in (a_set, d_set):
        for h in range(HI):
            finish(to_line(group, z, h, 0))
            finish(to_line(group, z, h, 1))
            finish(to_sibling(group, z, h))

        for c in range(1, CHUNKS):
            ring(group, c, 0, finish, False)
            ring(group, c, 1, finish, False)

    def drain(t, carry):
        x_copy(t).wait_send()
        for way in range(2):
            y_copy(t, way).wait_send()
            m_copy(t, way).wait_send()
            n_copy(t, way).wait_send()
            p_copy(t, way).wait_send()
        w_copy(t).wait_send()
        for h in range(HI):
            store(t, h).wait()
        for lane in range(7):
            c_copy(t, k, lane, partner).wait_send()
        return carry

    lax.fori_loop(0, CHUNKS // 2, drain, 0)
    for n, (target, slot) in enumerate(chip):
        spot = sg_chip.at[slot]
        remote(spot, spot, g_send.at[n], g_recv.at[slot], target).wait_recv()
    sg_line[z] = (sg_chip[0] + sg_chip[1]) + (sg_chip[2] + sg_chip[3])

    def line_copy(n, target):
        spot = sg_line.at[z]
        return remote(spot, spot, l_send.at[n], l_recv.at[z], target)

    for n, target in enumerate(line):
        line_copy(n, target).start()
    lax.fori_loop(CHUNKS // 2, CHUNKS, drain, 0)
    for n, target in enumerate(line):
        slot = lax.rem(z + 1 + n, Z)
        spot = sg_line.at[slot]
        remote(spot, spot, l_send.at[n], l_recv.at[slot], target).wait_recv()
    total = sg_line[0]
    for n in range(1, Z):
        total = total + sg_line[n]
    diag = lax.broadcasted_iota(jnp.int32, total.shape, 0) == lax.broadcasted_iota(jnp.int32, total.shape, 1)
    sig_ref[...] = jnp.sum(jnp.where(diag, total, 0.0), axis=0, keepdims=True)[:, : sig_ref.shape[1]]

    for n, (target, slot) in enumerate(chip):
        chip_copy(n, target).wait_send()
    for n, target in enumerate(line):
        line_copy(n, target).wait_send()


def hand_over(panel_in, sig_in, panel_out, sig_out):
    panel_out[...] = panel_in[...]
    sig_out[...] = sig_in[...]


def local(
    three_index,
    polar_prev,
    states,
    mo_energy,
    vir_energy,
    orbital_energy,
    occ_index,
    state_index,
    slab_rows,
):
    ri_count = lax.axis_size("ri")
    occ_count = lax.axis_size("occ")
    assert (ri_count, occ_count) == (HI * Z * CORE, LO * YS)
    p_dev = three_index.shape[0]
    col_block = polar_prev.shape[0]
    picks = slab_rows.shape[0] // ri_count
    ns_dev, orbitals = states.shape[1:]
    pairs = three_index.shape[1] * three_index.shape[2]
    spread = ns_dev * orbitals
    y_tiles = Y_FIRST
    x_tiles = p_dev // LANE - Y_FIRST

    def message(count, *lead):
        return pltpu.VMEM((CHUNKS, *lead, count + 1, HALF, LANE), jnp.int16)

    vmem = pl.BlockSpec(memory_space=pltpu.VMEM)
    hbm = pl.BlockSpec(memory_space=pl.ANY)
    smem = pl.BlockSpec(memory_space=pltpu.SMEM)
    dma = pltpu.SemaphoreType.DMA
    ring_sems = [dma((Z, HI)), dma((Z, HI)), dma((Z, HI, 3)), dma((1,))]
    panel_out, sig = pl.pallas_call(
        kernel,
        out_shape=(
            jax.ShapeDtypeStruct((col_block, p_dev), F32),
            jax.ShapeDtypeStruct((1, ns_dev), F32),
        ),
        in_specs=[hbm, hbm, hbm, vmem, vmem] + [smem] * 4,
        out_specs=(hbm, vmem),
        scratch_shapes=[
            pltpu.VMEM((Z, CORE, HI, picks, pairs), BF16),
            pltpu.VMEM((Z, CORE, HI, picks, spread), BF16),
            pltpu.VMEM((CHUNKS * occ_count, 2 * HALF, p_dev), F32),
            message(YS * 2 * x_tiles), message(YS * 2 * x_tiles),
            message(2 * x_tiles, 2), message(2 * x_tiles, 2),
            message(x_tiles, 2), message(x_tiles, 2),
            message(2 * LO * y_tiles, 2), message(2 * LO * y_tiles, 2),
            message(LO * y_tiles, 2), message(LO * y_tiles, 2),
            message(2 * y_tiles), message(2 * y_tiles),
            pltpu.VMEM((CHUNKS, occ_count, 2 * HALF, p_dev), BF16),
            pltpu.VMEM((8, spread), F32),
            pltpu.VMEM((HI * CORE, 8, LANE), F32),
            pltpu.VMEM((Z, 8, LANE), F32),
            pltpu.VMEM((p_dev, spread), BF16),
            pltpu.VMEM((LANE * ns_dev, LANE), F32),
            pltpu.VMEM((picks, spread), BF16),
            pltpu.VMEM((p_dev, ns_dev, orbitals), BF16),
            pltpu.VMEM((col_block, p_dev), F32),
            pltpu.VMEM((p_dev, pairs), BF16),
            pltpu.VMEM((three_index.shape[2] // LANE, picks, 8, LANE), F32),
            pltpu.VMEM((col_block, p_dev), F32),
            pltpu.VMEM(three_index.shape, BF16),
            *ring_sems,
            *ring_sems,
            dma((CHUNKS,)), dma((CHUNKS,)),
            dma((CHUNKS, 2)), dma((CHUNKS, 2)),
            dma((CHUNKS, 2)), dma((CHUNKS, 2)),
            dma((CHUNKS, 2)), dma((CHUNKS, 2)),
            dma((CHUNKS, 2)), dma((CHUNKS, 2)),
            dma((CHUNKS,)), dma((CHUNKS,)),
            dma((CHUNKS, 7)), dma((CHUNKS, occ_count)),
            dma((3,)), dma((HI * CORE,)),
            dma((Z - 1,)), dma((Z,)),
            dma((1,)), dma((1,)), dma((3,)), dma((CHUNKS, HI)),
        ],
        compiler_params=pltpu.CompilerParams(
            collective_id=0, has_side_effects=True, vmem_limit_bytes=60 * 2**20
        ),
        cost_estimate=pl.CostEstimate(
            flops=13 * 10**9, bytes_accessed=9 * 2**20, transcendentals=0
        ),
    )(
        three_index, states, polar_prev,
        vir_energy.reshape(1, -1), orbital_energy.reshape(1, -1),
        mo_energy, occ_index, state_index, slab_rows,
    )
    panel_out, sig = pl.pallas_call(
        hand_over,
        out_shape=(
            jax.ShapeDtypeStruct((col_block, p_dev), F32),
            jax.ShapeDtypeStruct((1, ns_dev), F32),
        ),
        in_specs=[vmem, vmem],
        out_specs=(vmem, vmem),
    )(panel_out, sig)
    return (panel_out, sig.reshape(ns_dev))


def solution(mesh):
    in_specs = (
        P("ri", "occ", None),
        P("occ", "ri"),
        P("ri", "occ", None),
        P(),
        P(),
        P(),
        P("occ"),
        P("occ"),
        P(),
    )
    out_specs = (P("occ", "ri"), P("occ"))
    return jax.shard_map(local, mesh=mesh, in_specs=in_specs, out_specs=out_specs, check_vma=False)
```

```python
import jax
import jax.numpy as jnp
from jax import lax
from jax.experimental import pallas as pl
from jax.experimental.pallas import tpu as pltpu
from jax.sharding import PartitionSpec as P

HI, Z, CORE, LO, YS = 2, 8, 2, 2, 4
CHUNKS = Z
LANE = 128
HALF = 16
PIECES = 4
VIA_X = (0, 1, 2, 3)
Y_FIRST = 4

(
    RELAY, A_OPP, D_PREP, D_OWN, D_OPP, A_RING, A_RING2, D_RING, D_RING2, PART_Y, PART_X, SUM, PASS, PASS_Y,
    SUM_Y, PANEL, NEAR, FAR_R, FAR_L, PAIRS, X_SPREAD, S_SPREAD,
) = range(22)
ORDER = (
    (D_PREP, 0), (X_SPREAD, 4), (S_SPREAD, 0), (X_SPREAD, 5), (X_SPREAD, 6), (X_SPREAD, 7), (X_SPREAD, 0),
    (X_SPREAD, 1), (A_RING, 1), (A_RING, 2), (X_SPREAD, 2), (X_SPREAD, 3), (A_OPP, 0), (S_SPREAD, 1),
    (RELAY, 0), (PART_Y, 0), (PART_X, 0), (S_SPREAD, 2), (A_RING, 3), (A_RING, 4), (S_SPREAD, 3),
    (A_RING2, 1), (A_RING2, 2), (PASS_Y, 0), (S_SPREAD, 4), (PART_Y, 1), (PART_Y, 2), (PART_X, 1),
    (PART_X, 2), (SUM, 0), (A_RING, 5), (A_RING2, 4), (S_SPREAD, 5), (A_RING2, 3), (PASS_Y, 1), (PASS_Y, 2),
    (SUM_Y, 0), (PASS, 0), (S_SPREAD, 6), (PART_Y, 3), (PART_Y, 4), (D_OWN, 0), (PART_X, 3), (PANEL, 0),
    (A_RING, 6), (PART_X, 4), (A_RING2, 6), (SUM, 1), (SUM, 2), (A_RING2, 5), (S_SPREAD, 7), (PASS_Y, 3),
    (D_OPP, 0), (SUM_Y, 1), (PART_Y, 5), (PART_Y, 6), (PART_X, 6), (PASS, 1), (A_RING, 7), (SUM_Y, 2),
    (PASS_Y, 4), (NEAR, 0), (PART_X, 5), (PASS, 2), (D_RING, 1), (SUM_Y, 3), (PANEL, 1), (PANEL, 2),
    (D_RING, 2), (A_RING2, 7), (SUM, 3), (PASS_Y, 5), (PASS_Y, 6), (PART_Y, 7), (SUM, 4), (SUM_Y, 4),
    (FAR_L, 0), (D_RING2, 1), (PART_X, 7), (PASS, 3), (D_RING2, 2), (SUM_Y, 6), (NEAR, 1), (FAR_R, 1),
    (PASS, 4), (NEAR, 2), (SUM_Y, 5), (SUM, 5), (D_RING, 3), (PANEL, 3), (FAR_R, 0), (PASS_Y, 7), (SUM, 6),
    (D_RING, 4), (PANEL, 4), (D_RING2, 4), (D_RING2, 3), (SUM, 7), (FAR_L, 1), (NEAR, 3), (PASS, 5),
    (PAIRS, 0, 0), (NEAR, 4), (PAIRS, 0, 1), (FAR_L, 2), (PASS, 6), (PAIRS, 0, 2), (SUM_Y, 7), (FAR_R, 3),
    (PAIRS, 0, 3), (PAIRS, 1, 0), (PAIRS, 1, 1), (PAIRS, 1, 2), (D_RING, 5), (PAIRS, 1, 3), (PANEL, 5),
    (PASS, 7), (FAR_R, 4), (D_RING, 6), (PANEL, 6), (D_RING2, 5), (NEAR, 5), (D_RING2, 6), (PANEL, 7),
    (FAR_L, 4), (FAR_R, 2), (NEAR, 6), (FAR_L, 3), (NEAR, 7), (PAIRS, 2, 0), (D_RING, 7), (PAIRS, 2, 1),
    (PAIRS, 2, 2), (FAR_R, 5), (FAR_L, 5), (PAIRS, 2, 3), (D_RING2, 7), (PAIRS, 3, 0), (PAIRS, 3, 1),
    (PAIRS, 3, 2), (PAIRS, 3, 3), (FAR_R, 6), (FAR_L, 6), (PAIRS, 4, 0), (PAIRS, 4, 1), (PAIRS, 4, 2),
    (PAIRS, 4, 3), (FAR_R, 7), (FAR_L, 7), (PAIRS, 5, 0), (PAIRS, 5, 1), (PAIRS, 5, 2), (PAIRS, 5, 3),
    (PAIRS, 6, 0), (PAIRS, 6, 1), (PAIRS, 6, 2), (PAIRS, 6, 3), (PAIRS, 7, 0), (PAIRS, 7, 1), (PAIRS, 7, 2),
    (PAIRS, 7, 3),
)

MESH = pl.DeviceIdType.MESH
F32 = jnp.float32
BF16 = jnp.bfloat16


def remote(src, dst, send_sem, recv_sem, target):
    return pltpu.make_async_remote_copy(
        src_ref=src, dst_ref=dst, send_sem=send_sem, recv_sem=recv_sem,
        device_id=target, device_id_type=MESH,
    )


def tile_scale(peak):
    return jnp.floor(jnp.log(jnp.maximum(peak, 1e-20) * 1.001) * 1.4426950408889634) + 1.0


def encode(blocks, message):
    peak = None
    for load in blocks:
        for lane in load.lanes:
            high = jnp.abs(load(lane))
            peak = high if peak is None else jnp.maximum(peak, high)
    exponent = tile_scale(peak)
    inverse = jnp.exp2(15.0 - exponent)
    at = 0
    for load in blocks:
        for lane in load.lanes:
            message[at] = (load(lane) * inverse).astype(jnp.int32).astype(jnp.int16)
            at += 1
    message[at] = exponent.astype(jnp.int32).astype(jnp.int16)


def unit(message, last):
    return jnp.exp2(message[last].astype(jnp.int32).astype(F32) - 15.0)


def decode(message, at, scale):
    return message[at].astype(jnp.int32).astype(F32) * scale


class Rows:
    def __init__(self, ref, block, first, lanes):
        self.ref, self.block, self.first, self.lanes = ref, block, first, lanes

    def __call__(self, lane):
        return self.ref[self.block, pl.ds(self.first, HALF), pl.ds(lane, LANE)]


def kernel(
    x3_hbm, s3_hbm, prev_hbm, vir_ref, orb_ref, mo_ref, occ_idx, state_idx, slab_rows,
    out_hbm, sig_ref,
    cols, slab, part, x_out, x_in, y_out, y_in, m_out, m_in, n_out, n_in, p_out, p_in, w_out, w_in,
    scr, acc, sg_chip, sg_line, s_ref, wide, relayed, s3_ref, prev_ref, x_ref, few, out_ref, x3_ref,
    a_recv, a_sib, a_send, a_opp, d_recv, d_sib, d_send, d_opp,
    x_send, x_recv, y_send, y_recv, m_send, m_recv, n_send, n_recv, p_send, p_recv, w_send, w_recv,
    c_send, c_recv, g_send, g_recv, l_send, l_recv, r_send, r_recv, load, done,
):
    width = prev_ref.shape[1]
    x_lanes = range(0, width - Y_FIRST * LANE, LANE)
    y_lanes = range(width - Y_FIRST * LANE, width, LANE)
    x_tiles, y_tiles = len(x_lanes), len(y_lanes)
    ri, k = lax.axis_index("ri"), lax.axis_index("occ")
    core = lax.rem(ri, CORE)
    z = lax.rem(ri // CORE, Z)
    hi = ri // (CORE * Z)
    y = lax.rem(k, YS)
    lo = k // YS
    xo = 1 - lo

    def ri_at(h, zz, c):
        return (h * Z + zz) * CORE + c

    def occ_at(x, yy):
        return x * YS + yy

    up = (ri_at(hi, lax.rem(z + 1, Z), core), k)
    down = (ri_at(hi, lax.rem(z + Z - 1, Z), core), k)
    sibling = (ri_at(hi, z, 1 - core), k)
    opposite = (ri_at(1 - hi, z, core), k)
    across = (ri_at(1 - hi, z, 1 - core), k)
    partner = (ri, occ_at(xo, y))
    diagonal = (ri_at(1 - hi, z, core), occ_at(xo, y))
    y_next, y_last, y_far = lax.rem(y + 1, YS), lax.rem(y + YS - 1, YS), lax.rem(y + 2, YS)
    right, left = (ri, occ_at(lo, y_next)), (ri, occ_at(lo, y_last))
    line = [(ri_at(hi, lax.rem(z + s, Z), core), k) for s in range(1, Z)]

    s3_copy = pltpu.make_async_copy(s3_hbm, s3_ref, load.at[0])
    prev_copy = pltpu.make_async_copy(prev_hbm, prev_ref, load.at[1])
    x3_copy = pltpu.make_async_copy(x3_hbm, x3_ref, load.at[2])
    x3_copy.start()
    barrier = pltpu.get_barrier_semaphore()
    friends = [sibling, opposite, across, partner, diagonal, right, left] + line
    for friend in friends:
        pl.semaphore_signal(barrier, inc=1, device_id=friend, device_id_type=MESH)

    x3_copy.wait()
    s3_copy.start()
    prev_copy.start()

    per_sub = prev_ref.shape[0] // (HI * Z * CORE)
    picks = LO * YS * per_sub
    pairs_in, virtual = x3_ref.shape[1:]
    local_rows = [
        lax.rem(slab_rows[kk * prev_ref.shape[0] + ri * per_sub + s], x3_ref.shape[0])
        for kk in range(LO * YS)
        for s in range(per_sub)
    ]
    few_rows = few.reshape(virtual // LANE, picks * 8, LANE)
    for j, row in enumerate(local_rows):
        raw = x3_ref[row].astype(F32)
        for lane in range(0, virtual, LANE):
            few[lane // LANE, j, pl.ds(0, pairs_in), :] = raw[:, lane : lane + LANE]
    for i in range(pairs_in):
        gap = vir_ref[...] - mo_ref[occ_idx[i]]
        weight = 4.0 * gap / (gap * gap + 0.25)
        for lane in range(0, virtual, LANE):
            picked = few_rows[lane // LANE, pl.ds(i, picks, stride=8), :]
            cols[z, core, hi, :, pl.ds(i * virtual + lane, LANE)] = (
                picked * weight[:, lane : lane + LANE]
            ).astype(BF16)

    pl.semaphore_wait(barrier, len(friends))

    a_set = (cols, a_recv, a_sib, a_send, a_opp)
    d_set = (slab, d_recv, d_sib, d_send, d_opp)

    def to_opposite(group):
        buf, recv, sib, send, opp = group
        shard = buf.at[z, core, hi]
        return remote(shard, shard, opp.at[0], recv.at[z, hi], opposite)

    def to_line(group, zz, h, way):
        buf, recv, sib, send, opp = group
        shard = buf.at[zz, core, h]
        return remote(shard, shard, send.at[zz, h, way], recv.at[zz, h], (up, down)[way])

    def to_sibling(group, zz, h):
        buf, recv, sib, send, opp = group
        shard = buf.at[zz, core, h]
        return remote(shard, shard, send.at[zz, h, 2], sib.at[zz, h], sibling)

    def await_shard(group, zz, h):
        buf, recv, sib, send, opp = group
        shard = buf.at[zz, core, h]
        remote(shard, shard, send.at[zz, h, 0], recv.at[zz, h], up).wait_recv()

    def await_sibling(group, zz):
        buf, recv, sib, send, opp = group
        for h in range(HI):
            shard = buf.at[zz, 1 - core, h]
            remote(shard, shard, send.at[zz, h, 2], sib.at[zz, h], sibling).wait_recv()

    def ring(group, c, far, act, arrive):
        zz = chunk_z(c)
        h = 1 - hi if far else hi
        way = (c + 1) % 2
        if arrive:
            await_shard(group, zz, h)
        if c < 5 or (c < 7 and way == far):
            act(to_line(group, zz, h, way))

        act(to_sibling(group, zz, h))

    def start(copy):
        copy.start()

    def finish(copy):
        copy.wait_send()

    def chunk_z(t):
        if isinstance(t, int):
            return lax.rem(z + (Z - (t + 1) // 2 if t % 2 else t // 2), Z)
        return lax.rem(z + jnp.where(lax.rem(t, 2) == 1, Z - (t + 1) // 2, t // 2), Z)

    def products(t, lanes):
        zz = chunk_z(t)
        shards = CORE * HI
        lhs = cols[zz].reshape(shards * picks, cols.shape[-1])
        step = 256
        for first in range(lanes.start, lanes.stop, step):
            res = lax.dot_general(
                lhs, x_ref[pl.ds(first, step), :], (((1,), (1,)), ((), ())),
                preferred_element_type=F32,
            )
            for kk in range(LO * YS):
                for g in range(shards):
                    part[t * (LO * YS) + kk, pl.ds(g * 8, 8), pl.ds(first, step)] = res[
                        g * picks + kk * 8 : g * picks + kk * 8 + 8
                    ]

    def part_y(t):
        await_sibling(a_set, chunk_z(t))
        products(t, y_lanes)
        for way in range(2):
            beside = (y_next, y_last)[way]
            blocks = [Rows(part, at(t, lx, y_far), way * HALF, y_lanes) for lx in range(LO)]
            blocks += [Rows(part, at(t, lx, beside), (1 - way) * HALF, y_lanes) for lx in range(LO)]
            encode(blocks, n_out.at[t, way])
            n_copy(t, way).start()

    def part_x(t):
        products(t, x_lanes)
        blocks = []
        for yy in range(YS):
            for first in (0, HALF):
                blocks.append(Rows(part, at(t, xo, yy), first, x_lanes))
        encode(blocks, x_out.at[t])
        x_copy(t).start()

    def n_copy(t, way):
        return remote(
            n_out.at[t, way], n_in.at[t, way], n_send.at[t, way], n_recv.at[t, way], (right, left)[way]
        )

    def p_copy(t, way):
        return remote(
            p_out.at[t, way], p_in.at[t, way], p_send.at[t, way], p_recv.at[t, way], (right, left)[way]
        )

    def w_copy(t):
        return remote(w_out.at[t], w_in.at[t], w_send.at[t], w_recv.at[t], partner)

    def x_copy(t):
        return remote(x_out.at[t], x_in.at[t], x_send.at[t], x_recv.at[t], partner)

    def y_copy(t, way):
        return remote(
            y_out.at[t, way], y_in.at[t, way], y_send.at[t, way], y_recv.at[t, way], (right, left)[way]
        )

    def m_copy(t, way):
        return remote(
            m_out.at[t, way], m_in.at[t, way], m_send.at[t, way], m_recv.at[t, way], (right, left)[way]
        )

    def c_copy(t, block, lane, target):
        spot = scr.at[t, block]
        return remote(spot, spot, c_send.at[t, lane], c_recv.at[t, block], target)

    def at(t, lx, yy):
        return t * (LO * YS) + occ_at(lx, yy)

    def add(block, first, lanes, message, tile, scale):
        for lane in lanes:
            spot = (block, pl.ds(first, HALF), pl.ds(lane, LANE))
            part[spot] = part[spot] + decode(message, tile, scale)
            tile += 1

    def pair_sum(t):
        x_copy(t).wait_recv()
        message = x_in.at[t]
        scale = unit(message, YS * 2 * x_tiles)
        for yy in range(YS):
            for half in range(2):
                add(at(t, lo, yy), half * HALF, x_lanes, message, (yy * 2 + half) * x_tiles, scale)
        for way in range(2):
            beside = (y_next, y_last)[way]
            encode(
                [
                    Rows(part, at(t, lo, y_far), way * HALF, x_lanes),
                    Rows(part, at(t, lo, beside), (1 - way) * HALF, x_lanes),
                ],
                y_out.at[t, way],
            )
            y_copy(t, way).start()

    def pass_on(t):
        for way in range(2):
            beside = (y_next, y_last)[way]
            y_copy(t, way).wait_recv()
            message = y_in.at[t, way]
            add(at(t, lo, beside), way * HALF, x_lanes, message, 0, unit(message, 2 * x_tiles))
            encode([Rows(part, at(t, lo, beside), way * HALF, x_lanes)], m_out.at[t, way])
            m_copy(t, way).start()

    def pass_on_y(t):
        for way in range(2):
            beside = (y_next, y_last)[way]
            n_copy(t, way).wait_recv()
            message = n_in.at[t, way]
            scale = unit(message, 2 * LO * y_tiles)
            for lx in range(LO):
                add(at(t, lx, beside), way * HALF, y_lanes, message, lx * y_tiles, scale)
            encode(
                [Rows(part, at(t, lx, beside), way * HALF, y_lanes) for lx in range(LO)], p_out.at[t, way]
            )
            p_copy(t, way).start()

    def sum_y(t):
        for way in range(2):
            p_copy(t, way).wait_recv()
        for half in range(2):
            near, far = n_in.at[t, 1 - half], p_in.at[t, half]
            near_scale, far_scale = unit(near, 2 * LO * y_tiles), unit(far, LO * y_tiles)
            for lx in range(LO):
                add(at(t, lx, y), half * HALF, y_lanes, near, (LO + lx) * y_tiles, near_scale)
                add(at(t, lx, y), half * HALF, y_lanes, far, lx * y_tiles, far_scale)
        encode([Rows(part, at(t, xo, y), half * HALF, y_lanes) for half in range(2)], w_out.at[t])
        w_copy(t).start()

    def panel(t):
        zz = chunk_z(t)
        for way in range(2):
            m_copy(t, way).wait_recv()
        w_copy(t).wait_recv()
        if t == 0:
            prev_copy.wait()
        other = w_in.at[t]
        other_scale = unit(other, 2 * y_tiles)
        for half in range(2):
            near, far = y_in.at[t, 1 - half], m_in.at[t, half]
            near_scale, far_scale = unit(near, 2 * x_tiles), unit(far, x_tiles)
            for lane in range(0, width, LANE):
                total = part[at(t, lo, y), pl.ds(half * HALF, HALF), pl.ds(lane, LANE)]
                tile = lane // LANE
                if tile < x_tiles:
                    total = total + decode(near, x_tiles + tile, near_scale)
                    total = total + decode(far, tile, far_scale)
                else:
                    total = total + decode(other, half * y_tiles + tile - x_tiles, other_scale)
                kept = []
                for h in range(HI):
                    row = pl.multiple_of(h * (Z * CORE * 8) + zz * (CORE * 8) + half * 8, 8)
                    value = prev_ref[pl.ds(row, 8), pl.ds(lane, LANE)] - total[h * 8 : h * 8 + 8]
                    out_ref[pl.ds(row, 8), pl.ds(lane, LANE)] = value
                    kept.append(value)
                scr[t, k, pl.ds(half * HALF, HALF), pl.ds(lane, LANE)] = jnp.concatenate(
                    kept, axis=0
                ).astype(BF16)
        for h in range(HI):
            store(t, h).start()
        c_copy(t, k, 0, partner).start()
        c_copy(t, k, 1, right).start()
        c_copy(t, k, 2, left).start()

    def store(t, h):
        deep = CORE * 8
        rows = pl.ds(pl.multiple_of((h * Z + chunk_z(t)) * deep, deep), deep)
        return pltpu.make_async_copy(out_ref.at[rows], out_hbm.at[rows], done.at[t, h])

    def await_block(t, block):
        c_copy(t, block, 0, partner).wait_recv()

    def spread_partner(t):
        block = occ_at(xo, y)
        await_block(t, block)
        c_copy(t, block, 3, right).start()
        c_copy(t, block, 4, left).start()

    def spread_right(t):
        if t in VIA_X and t % 2 == 0:
            block, target = occ_at(xo, y_far), partner
        else:
            block, target = occ_at(lo, y_last), right
        await_block(t, block)
        c_copy(t, block, 5, target).start()

    def spread_left(t):
        if t in VIA_X and t % 2 == 1:
            block, target = occ_at(lo, y_far), partner
        else:
            block, target = occ_at(xo, y_next), left
        await_block(t, block)
        c_copy(t, block, 6, target).start()

    def rest(t):
        blocks = [occ_at(xo, y_last), occ_at(lo, y_next)]
        if t in VIA_X and t % 2 == 0:
            blocks += [occ_at(lo, y_last), occ_at(lo, y_far)]
        elif t in VIA_X:
            blocks += [occ_at(xo, y_next), occ_at(xo, y_far)]
        else:
            blocks += [occ_at(lo, y_far), occ_at(xo, y_far)]
        return blocks

    def energy(t, quarter):
        zz = chunk_z(t)
        if quarter == 0:
            for block in rest(t):
                await_block(t, block)
            await_sibling(d_set, zz)
        lhs = scr[t].reshape(LO * YS * 2 * HALF, width)
        step = s_ref.shape[1] // 4
        lanes = pl.ds(quarter * step, step)
        applied = jnp.dot(lhs, s_ref[:, lanes], preferred_element_type=F32)
        total = acc[:, lanes]
        for g in range(CORE * HI):
            rows = slab[zz, g // HI, g % HI, :, lanes].astype(F32)
            for kk in range(LO * YS):
                spot = kk * 2 * HALF + g * 8
                total = total + applied[spot : spot + 8] * rows[kk * 8 : kk * 8 + 8]
        acc[:, lanes] = total

    start(to_opposite(a_set))
    start(to_line(a_set, z, hi, 0))
    start(to_line(a_set, z, hi, 1))
    start(to_sibling(a_set, z, hi))

    depth = wide.shape[0] // 8
    wide_rows = wide.reshape(depth, 8, LANE)

    def spread_block(n):
        at_row = n * depth
        for lane in range(0, virtual, LANE):
            wide_rows[:, pl.ds(0, pairs_in), :] = x3_ref[pl.ds(at_row, depth), :, pl.ds(lane, LANE)].astype(F32)
            for i in range(pairs_in):
                x_ref[pl.ds(at_row, depth), pl.ds(i * virtual + lane, LANE)] = wide[
                    pl.ds(i, depth, stride=8), :
                ].astype(BF16)

    acc[...] = jnp.zeros_like(acc)

    def to_diagonal():
        return remote(slab.at[z, core, hi], relayed, r_send.at[0], r_recv.at[0], diagonal)

    def relay_on():
        return remote(relayed, slab.at[z, core, 1 - hi], d_opp.at[0], d_recv.at[z, 1 - hi], partner)

    states, orbitals = s3_ref.shape[1:]
    assert states == 8

    def prepare_states(t):
        s3_copy.wait()
        for j, row in enumerate(local_rows):
            raw = s3_ref[row].astype(F32)
            for lane in range(0, orbitals, LANE):
                few[lane // LANE, j] = raw[:, lane : lane + LANE]
        for state in range(states):
            for lane in range(0, orbitals, LANE):
                slab[z, core, hi, :, pl.ds(state * orbitals + lane, LANE)] = few_rows[
                    lane // LANE, pl.ds(state, picks, stride=8), :
                ].astype(BF16)
        start(to_diagonal())

    def spread_states(n):
        at_row = n * depth
        for lane in range(0, orbitals, LANE):
            raw = s3_ref[pl.ds(at_row, depth), :, pl.ds(lane, LANE)].astype(F32)
            wide[...] = raw.reshape(depth * states, LANE)
            for state in range(states):
                s_ref[pl.ds(at_row, depth), pl.ds(state * orbitals + lane, LANE)] = wide[
                    pl.ds(state, depth, stride=states), :
                ].astype(BF16)

    def relay(t):
        to_diagonal().wait_recv()
        start(relay_on())

    def first_far(group):
        await_shard(group, z, 1 - hi)
        start(to_sibling(group, z, 1 - hi))
        start(to_line(group, z, 1 - hi, 0))
        start(to_line(group, z, 1 - hi, 1))

    def first_own(t):
        start(to_sibling(d_set, z, hi))
        start(to_line(d_set, z, hi, 0))
        start(to_line(d_set, z, hi, 1))

    stages = {
        RELAY: relay,
        A_OPP: lambda t: first_far(a_set),
        D_OWN: first_own,
        D_OPP: lambda t: first_far(d_set),
        A_RING: lambda t: ring(a_set, t, 0, start, True),
        A_RING2: lambda t: ring(a_set, t, 1, start, True),
        D_RING: lambda t: ring(d_set, t, 0, start, True),
        D_RING2: lambda t: ring(d_set, t, 1, start, True),
        D_PREP: prepare_states,
        X_SPREAD: spread_block,
        S_SPREAD: spread_states,
        PART_Y: part_y,
        PART_X: part_x,
        SUM: pair_sum,
        PASS: pass_on,
        PASS_Y: pass_on_y,
        SUM_Y: sum_y,
        PANEL: panel,
        NEAR: spread_partner,
        FAR_R: spread_right,
        FAR_L: spread_left,
        PAIRS: energy,
    }

    for stage, *spot in ORDER:
        stages[stage](*spot)

    pairs = jnp.sum(acc[...], axis=0, keepdims=True)
    mine = hi * CORE + core
    for n in range(state_idx.shape[0]):
        gap = mo_ref[state_idx[n]] - orb_ref[...]
        factor = gap / (gap * gap + 0.25)
        value = jnp.sum(factor * pairs[:, n * orbitals : (n + 1) * orbitals], axis=1, keepdims=True)
        sg_chip[mine, pl.ds(n, 1), :] = jnp.broadcast_to(value, (1, LANE))

    def chip_copy(n, target):
        spot = sg_chip.at[mine]
        return remote(spot, spot, g_send.at[n], g_recv.at[mine], target)

    chip = [
        (sibling, hi * CORE + 1 - core),
        (opposite, (1 - hi) * CORE + core),
        (across, (1 - hi) * CORE + 1 - core),
    ]
    for n, (target, slot) in enumerate(chip):
        chip_copy(n, target).start()
    finish(to_opposite(a_set))
    finish(to_diagonal())
    finish(relay_on())
    for group in (a_set, d_set):
        for h in range(HI):
            finish(to_line(group, z, h, 0))
            finish(to_line(group, z, h, 1))
            finish(to_sibling(group, z, h))

        for c in range(1, CHUNKS):
            ring(group, c, 0, finish, False)
            ring(group, c, 1, finish, False)

    def drain(t, carry):
        x_copy(t).wait_send()
        for way in range(2):
            y_copy(t, way).wait_send()
            m_copy(t, way).wait_send()
            n_copy(t, way).wait_send()
            p_copy(t, way).wait_send()
        w_copy(t).wait_send()
        for h in range(HI):
            store(t, h).wait()
        for lane in range(7):
            c_copy(t, k, lane, partner).wait_send()
        return carry

    lax.fori_loop(0, CHUNKS // 2, drain, 0)
    for n, (target, slot) in enumerate(chip):
        spot = sg_chip.at[slot]
        remote(spot, spot, g_send.at[n], g_recv.at[slot], target).wait_recv()
    sg_line[z] = (sg_chip[0] + sg_chip[1]) + (sg_chip[2] + sg_chip[3])

    def line_copy(n, target):
        spot = sg_line.at[z]
        return remote(spot, spot, l_send.at[n], l_recv.at[z], target)

    for n, target in enumerate(line):
        line_copy(n, target).start()
    lax.fori_loop(CHUNKS // 2, CHUNKS, drain, 0)
    for n, target in enumerate(line):
        slot = lax.rem(z + 1 + n, Z)
        spot = sg_line.at[slot]
        remote(spot, spot, l_send.at[n], l_recv.at[slot], target).wait_recv()
    total = sg_line[0]
    for n in range(1, Z):
        total = total + sg_line[n]
    diag = lax.broadcasted_iota(jnp.int32, total.shape, 0) == lax.broadcasted_iota(jnp.int32, total.shape, 1)
    sig_ref[...] = jnp.sum(jnp.where(diag, total, 0.0), axis=0, keepdims=True)[:, : sig_ref.shape[1]]

    for n, (target, slot) in enumerate(chip):
        chip_copy(n, target).wait_send()
    for n, target in enumerate(line):
        line_copy(n, target).wait_send()


def hand_over(panel_in, sig_in, panel_out, sig_out, held, in_sems, out_sems):
    deep = panel_in.shape[0] // PIECES
    loads, stores = [], []
    for n in range(PIECES):
        rows = pl.ds(n * deep, deep)
        loads.append(pltpu.make_async_copy(panel_in.at[rows], held.at[rows], in_sems.at[n]))
        stores.append(pltpu.make_async_copy(held.at[rows], panel_out.at[rows], out_sems.at[n]))
        loads[n].start()
    sig_out[...] = sig_in[...]
    for n in range(PIECES):
        loads[n].wait()
        stores[n].start()
    for copy in stores:
        copy.wait()


def local(
    three_index,
    polar_prev,
    states,
    mo_energy,
    vir_energy,
    orbital_energy,
    occ_index,
    state_index,
    slab_rows,
):
    ri_count = lax.axis_size("ri")
    occ_count = lax.axis_size("occ")
    assert (ri_count, occ_count) == (HI * Z * CORE, LO * YS)
    p_dev = three_index.shape[0]
    col_block = polar_prev.shape[0]
    picks = slab_rows.shape[0] // ri_count
    ns_dev, orbitals = states.shape[1:]
    pairs = three_index.shape[1] * three_index.shape[2]
    spread = ns_dev * orbitals
    y_tiles = Y_FIRST
    x_tiles = p_dev // LANE - Y_FIRST

    def message(count, *lead):
        return pltpu.VMEM((CHUNKS, *lead, count + 1, HALF, LANE), jnp.int16)

    vmem = pl.BlockSpec(memory_space=pltpu.VMEM)
    hbm = pl.BlockSpec(memory_space=pl.ANY)
    smem = pl.BlockSpec(memory_space=pltpu.SMEM)
    dma = pltpu.SemaphoreType.DMA
    ring_sems = [dma((Z, HI)), dma((Z, HI)), dma((Z, HI, 3)), dma((1,))]
    panel_out, sig = pl.pallas_call(
        kernel,
        out_shape=(
            jax.ShapeDtypeStruct((col_block, p_dev), F32),
            jax.ShapeDtypeStruct((1, ns_dev), F32),
        ),
        in_specs=[hbm, hbm, hbm, vmem, vmem] + [smem] * 4,
        out_specs=(hbm, vmem),
        scratch_shapes=[
            pltpu.VMEM((Z, CORE, HI, picks, pairs), BF16),
            pltpu.VMEM((Z, CORE, HI, picks, spread), BF16),
            pltpu.VMEM((CHUNKS * occ_count, 2 * HALF, p_dev), F32),
            message(YS * 2 * x_tiles), message(YS * 2 * x_tiles),
            message(2 * x_tiles, 2), message(2 * x_tiles, 2),
            message(x_tiles, 2), message(x_tiles, 2),
            message(2 * LO * y_tiles, 2), message(2 * LO * y_tiles, 2),
            message(LO * y_tiles, 2), message(LO * y_tiles, 2),
            message(2 * y_tiles), message(2 * y_tiles),
            pltpu.VMEM((CHUNKS, occ_count, 2 * HALF, p_dev), BF16),
            pltpu.VMEM((8, spread), F32),
            pltpu.VMEM((HI * CORE, 8, LANE), F32),
            pltpu.VMEM((Z, 8, LANE), F32),
            pltpu.VMEM((p_dev, spread), BF16),
            pltpu.VMEM((LANE * ns_dev, LANE), F32),
            pltpu.VMEM((picks, spread), BF16),
            pltpu.VMEM((p_dev, ns_dev, orbitals), BF16),
            pltpu.VMEM((col_block, p_dev), F32),
            pltpu.VMEM((p_dev, pairs), BF16),
            pltpu.VMEM((three_index.shape[2] // LANE, picks, 8, LANE), F32),
            pltpu.VMEM((col_block, p_dev), F32),
            pltpu.VMEM(three_index.shape, BF16),
            *ring_sems,
            *ring_sems,
            dma((CHUNKS,)), dma((CHUNKS,)),
            dma((CHUNKS, 2)), dma((CHUNKS, 2)),
            dma((CHUNKS, 2)), dma((CHUNKS, 2)),
            dma((CHUNKS, 2)), dma((CHUNKS, 2)),
            dma((CHUNKS, 2)), dma((CHUNKS, 2)),
            dma((CHUNKS,)), dma((CHUNKS,)),
            dma((CHUNKS, 7)), dma((CHUNKS, occ_count)),
            dma((3,)), dma((HI * CORE,)),
            dma((Z - 1,)), dma((Z,)),
            dma((1,)), dma((1,)), dma((3,)), dma((CHUNKS, HI)),
        ],
        compiler_params=pltpu.CompilerParams(
            collective_id=0, has_side_effects=True, vmem_limit_bytes=60 * 2**20
        ),
        cost_estimate=pl.CostEstimate(
            flops=13 * 10**9, bytes_accessed=9 * 2**20, transcendentals=0
        ),
    )(
        three_index, states, polar_prev,
        vir_energy.reshape(1, -1), orbital_energy.reshape(1, -1),
        mo_energy, occ_index, state_index, slab_rows,
    )
    panel_out, sig = pl.pallas_call(
        hand_over,
        out_shape=(
            jax.ShapeDtypeStruct((col_block, p_dev), F32),
            jax.ShapeDtypeStruct((1, ns_dev), F32),
        ),
        in_specs=[hbm, vmem],
        out_specs=(hbm, vmem),
        scratch_shapes=[pltpu.VMEM((col_block, p_dev), F32), dma((PIECES,)), dma((PIECES,))],
    )(panel_out, sig)
    return (panel_out, sig.reshape(ns_dev))


def solution(mesh):
    in_specs = (
        P("ri", "occ", None),
        P("occ", "ri"),
        P("ri", "occ", None),
        P(),
        P(),
        P(),
        P("occ"),
        P("occ"),
        P(),
    )
    out_specs = (P("occ", "ri"), P("occ"))
    return jax.shard_map(local, mesh=mesh, in_specs=in_specs, out_specs=out_specs, check_vma=False)
```
